256 devices in a mesh: ctx: 16 (over z_hi, y, core), ep: 16 (over z_lo, x).
Axes of the slice: x: 4, y: 4, z: 8 (z_hi: 2, z_lo: 4; z = z_hi * 4 + z_lo), core: 2. Of those that a mesh axis runs over, the one named last changes fastest.
Arguments:
- prompt_query: bfloat16 [16, 1024, 64, 512], P('ep', 'ctx'), may hold values from -6 to 6
- prompt_query_pos: bfloat16 [16, 1024, 4096], P('ep', 'ctx'), may hold values from -80 to 80
- prompt_latent: bfloat16 [16, 1024, 512], P('ep', 'ctx'), may hold values from -6 to 6
- prompt_pos: bfloat16 [16, 1024, 64], P('ep', 'ctx'), may hold values from -6 to 6
- decode_query: bfloat16 [16, 16, 2, 64, 512], P('ep', 'ctx'), may hold values from -6 to 6
- decode_query_pos: bfloat16 [16, 16, 2, 4096], P('ep', 'ctx'), may hold values from -80 to 80
- decode_latent: bfloat16 [16, 16, 2, 512], P('ep', 'ctx'), may hold values from -12 to 12
- decode_pos: bfloat16 [16, 16, 2, 64], P('ep', 'ctx'), may hold values from -12 to 12
- decode_hidden: bfloat16 [16, 16, 2, 3584], P('ep', 'ctx'), may hold values from -6 to 6
- norm_gain: bfloat16 [3584], replicated, may hold values from 0.25 to 1.75
- value_up: bfloat16 [64, 512, 128], P('ctx'), may hold values from -0.25 to 0.25
- out_proj: bfloat16 [8192, 3584], P('ctx'), may hold values from -0.0625 to 0.0625
- route_ids: int32 [16, 16, 2, 8], P('ep', 'ctx'), may hold values from 0 to 15, all different within a row; in each aligned block of 2 rows (0 to 1, 2 to 3, ..., all dimensions but the last counted through in order) at most 2 rows name the same one
- route_gates: bfloat16 [16, 16, 2, 8], P('ep', 'ctx'), may hold values from 0.049804688 to 1
- expert_gate: bfloat16 [16, 3584, 2048], P('ep', None, 'ctx'), may hold values from -0.09375 to 0.09375
- expert_up: bfloat16 [16, 3584, 2048], P('ep', None, 'ctx'), may hold values from -0.09375 to 0.09375
- expert_down: bfloat16 [16, 2048, 3584], P('ep', None, 'ctx'), may hold values from -0.125 to 0.125
Outputs:
- prefill_out: bfloat16 [16, 1024, 64, 512], P('ep', 'ctx')
- decode_out: bfloat16 [16, 16, 2, 3584], P('ep', 'ctx')
The draws below stay inside these ranges and needn't reach their ends.
Inputs may be any that keep to these rules, and one draw needn't show every extreme that they name: `route_ids`: each token names 8 different experts; every expert is named by some token.
All inputs are finite; a program needn't handle non-finite values.
Results may differ from the reference program's by a relative error of at most 0.03.
Values may be sent and summed in bfloat16 or wider, within the bound.
No kernel may reach another device: no remote copies, remote signals or barrier semaphores. Data moves between devices by JAX's collectives and lax.ppermute only.
A program may use at most 128 MiB of HBM per device.

```python
import math
import jax
import jax.numpy as jnp
import numpy as np
from jax import lax

D = 3584
HEADS = 64
LAT = 512
ROPE = 64
HV = 128
FF = 2048
TOPK = 8
STEPS = 2
LEN = 1024
SAMPLES = 16
GROUPS = 16
EXPERTS = 16


def rope_normal(key):
    return jnp.clip(jax.random.normal(key, (GROUPS, LEN, ROPE), jnp.float32), -6.0, 6.0)


def draw_prompt_pos(key, part):
    normal_part = rope_normal(key)
    result = normal_part
    return result.astype(jnp.bfloat16)


def draw_prompt_query_pos(key, part):
    key = jax.random.fold_in(key, 22)
    key_one = jax.random.fold_in(key, 0)
    shape = (GROUPS, LEN, HEADS, ROPE)
    result = jnp.clip(jax.random.normal(key_one, shape, jnp.float32), -6.0, 6.0)
    return result.reshape(GROUPS, LEN, HEADS * ROPE).astype(jnp.bfloat16)


def draw_prompt_query(key, part):
    key = jax.random.fold_in(key, 23)
    shape = (GROUPS, LEN, HEADS, LAT)
    result = jnp.clip(jax.random.normal(key, shape, jnp.float32), -6.0, 6.0)
    return result.astype(jnp.bfloat16)


def draw_decode_query_pos(key, part):
    key = jax.random.fold_in(key, 24)
    key_one = jax.random.fold_in(key, 0)
    shape = (GROUPS, SAMPLES, STEPS, HEADS, ROPE)
    result = jnp.clip(jax.random.normal(key_one, shape, jnp.float32), -6.0, 6.0)
    return result.reshape(GROUPS, SAMPLES, STEPS, HEADS * ROPE).astype(jnp.bfloat16)


def draw_decode_query(key, part):
    key = jax.random.fold_in(key, 25)
    shape = (GROUPS, SAMPLES, STEPS, HEADS, LAT)
    result = jnp.clip(jax.random.normal(key, shape, jnp.float32), -6.0, 6.0)
    return result.astype(jnp.bfloat16)


def draw_decode_hidden(key, part):
    key = jax.random.fold_in(key, 26)
    key_one, key_two, key_three = jax.random.split(key, 3)
    shape = (GROUPS, SAMPLES, STEPS, D)
    columns = jnp.exp(jax.random.uniform(key_two, (D,), jnp.float32, 0.0, 2.3))
    row_scale = jnp.exp(jax.random.uniform(key_three, (GROUPS, SAMPLES, STEPS, 1), jnp.float32, 0.0, 1.1))
    result = jnp.clip(jax.random.normal(key_one, shape, jnp.float32), -6.0, 6.0)
    return (0.03 * result * columns * row_scale).astype(jnp.bfloat16)


def levels(own_key, shape, shards, least, high):
    level, own = 1.0, jax.random.fold_in(own_key, 6)
    for dim, shards_of in shards:
        steps = jnp.exp(jax.random.uniform(jax.random.fold_in(own, dim), (shards_of,), jnp.float32, least / len(shards), high / len(shards)))
        level = level * jnp.repeat(steps, shape[dim] // shards_of).reshape([-1 if axis == dim else 1 for axis in range(len(shape))])
    return level


def deal_out(own_key, own, number, rows, count, top, reach, lean):
    ranking = jax.random.permutation(own_key, count)
    packed, ordinary = portions_of(count, rows * top, reach, lean, True), portions_of(count, rows * top, reach, lean, False)
    places = jnp.arange(count)

    def named(tallies, turn):
        used = int((tallies > 0).sum())
        fixed = max(1, used // 4)
        passed = fixed + (places - fixed + turn * (used - fixed)) % max(1, count - fixed)
        return jnp.zeros((count,), jnp.int32).at[ranking[jnp.where(places < fixed, places, passed)]].set(jnp.asarray(tallies, jnp.int32))

    tallies = jnp.where(number % 4 == 0, named(packed, number // 4), named(ordinary, number - number // 4 - 1))
    mixed = jax.random.permutation(jax.random.fold_in(own, 3), count)
    source_of, sink = mixed[0:count // 2 * 2:2], mixed[1:count // 2 * 2:2]
    margin = jnp.minimum(tallies[source_of] - 1, reach - tallies[sink]) // 2
    margin = jnp.where((source_of == ranking[0]) | (sink == ranking[0]) | (tallies[sink] == 0), 0, jnp.maximum(margin, 0))
    passed = jax.random.randint(jax.random.fold_in(own, 4), (count // 2,), 0, 1 << 20) % (margin + 1)
    tallies = tallies.at[source_of].add(-passed).at[sink].add(passed)
    members = jnp.searchsorted(jnp.cumsum(tallies), jnp.arange(rows * top), side="right").astype(jnp.int32)
    grid = members.reshape(top, rows).T
    grid = grid[jax.random.permutation(jax.random.fold_in(own, 1), rows)]
    turn = jax.random.randint(jax.random.fold_in(own, 2), (rows, 1), 0, top)
    return jnp.take_along_axis(grid, (jnp.arange(top)[None, :] + turn) % top, axis=1)


def portions_of(count, total, limit, lean, full):
    portions = [(1 << 20) // math.isqrt(standing ** lean) + 1 for standing in range(1, count + 1)]
    largest = limit if full else min(limit, max(-(-total // count), total * portions[0] // sum(portions)))
    least = 1 if total - largest >= count - 1 else 0
    given, surplus = [largest] + [least] * (count - 1), total - largest - least * (count - 1)
    while surplus > 0:
        free = [i for i in range(1, count) if given[i] < largest] or [i for i in range(1, count) if given[i] < limit]
        mass, left = sum([portions[i] for i in free]), surplus
        for i in free:
            addition = min(limit - given[i], max(1, left * portions[i] // mass), surplus)
            given[i] = given[i] + addition
            surplus = surplus - addition
    return np.array(given)


def centred(key, shape, spread, bound, shards=(), kind=jnp.bfloat16):
    array = jax.random.normal(key, shape, jnp.float32) * spread
    if len(shards) > 0:
        array = levels(key, shape, shards, -0.22, 0.18) * array
    return jnp.clip(array, min=-bound, max=bound).astype(kind)


def setup_inputs(seed: int = 0) -> dict:
    splits = jax.random.split(jax.random.key(seed), 18)
    prompt_query = draw_prompt_query(jax.random.fold_in(splits[17], 71), 0)
    prompt_query_pos = draw_prompt_query_pos(jax.random.fold_in(splits[17], 71), 0)
    prompt_latent = centred(splits[2], (GROUPS, LEN, LAT), 1.0, 6.0, ((0, 16), (1, 16)))
    prompt_pos = draw_prompt_pos(jax.random.fold_in(splits[17], 71), 0)
    decode_query = draw_decode_query(jax.random.fold_in(splits[17], 71), 0)
    decode_query_pos = draw_decode_query_pos(jax.random.fold_in(splits[17], 71), 0)
    decode_latent = centred(splits[6], (GROUPS, SAMPLES, STEPS, LAT), 2.0, 12.0, ((0, 16), (1, 16)))
    decode_pos = centred(splits[7], (GROUPS, SAMPLES, STEPS, ROPE), 2.0, 12.0, ((0, 16), (1, 16)))
    decode_hidden = draw_decode_hidden(jax.random.fold_in(splits[17], 71), 0)
    norm_gain = jnp.clip(1.0 + 0.15 * jax.random.normal(splits[9], (D,), jnp.float32), 0.25, 1.75).astype(jnp.bfloat16)
    value_up = centred(splits[10], (HEADS, LAT, HV), LAT ** -0.5, 0.25, ((0, 16),))
    out_proj = centred(splits[11], (HEADS * HV, D), (HEADS * HV) ** -0.5, 0.0625, ((0, 16),))
    route_ids_keys = jax.random.split(jax.random.fold_in(splits[12], 1), GROUPS * SAMPLES * STEPS // STEPS)
    route_ids_turns = jax.random.permutation(jax.random.fold_in(splits[12], 3), GROUPS * SAMPLES * STEPS // STEPS)
    route_ids = jax.vmap(lambda own, number: deal_out(jax.random.fold_in(splits[12], 2), own, number, STEPS, EXPERTS, TOPK, STEPS, 2))(route_ids_keys, route_ids_turns).reshape((GROUPS, SAMPLES, STEPS, TOPK))
    route_gates = jnp.clip(jnp.exp(math.log(1.0) - 2.9996462 * jax.random.uniform(splits[13], (GROUPS, SAMPLES, STEPS, TOPK), jnp.float32) ** levels(splits[13], (GROUPS, SAMPLES, STEPS, TOPK), ((0, 16), (1, 16)), -0.2, 0.2)), 0.049804688, 1.0).astype(jnp.bfloat16)
    expert_gate = centred(splits[14], (EXPERTS, D, FF), D ** -0.5, 0.09375, ((0, 16), (2, 16)))
    expert_up = centred(splits[15], (EXPERTS, D, FF), D ** -0.5, 0.09375, ((0, 16), (2, 16)))
    expert_down = centred(splits[16], (EXPERTS, FF, D), FF ** -0.5, 0.125, ((0, 16), (2, 16)))
    return {"prompt_query": prompt_query, "prompt_query_pos": prompt_query_pos, "prompt_latent": prompt_latent, "prompt_pos": prompt_pos, "decode_query": decode_query, "decode_query_pos": decode_query_pos, "decode_latent": decode_latent, "decode_pos": decode_pos, "decode_hidden": decode_hidden, "norm_gain": norm_gain, "value_up": value_up, "out_proj": out_proj, "route_ids": route_ids, "route_gates": route_gates, "expert_gate": expert_gate, "expert_up": expert_up, "expert_down": expert_down}


SOFTMAX_SCALE = 192.0 ** (-0.5)
MASK_VALUE = -1e+30
NORM_EPS = 1e-06
ROUTE_SCALE = 2.5

def prefill_group(inputs):
    query_lat, query_pos, key_lat, key_pos = inputs
    query_pos = query_pos.reshape(LEN, HEADS, ROPE)
    scores = jnp.einsum('pha,ja->phj', query_lat.astype(jnp.float32), key_lat.astype(jnp.float32))
    scores = scores + jnp.einsum('phb,jb->phj', query_pos.astype(jnp.float32), key_pos.astype(jnp.float32))
    scores = scores * SOFTMAX_SCALE
    positions = jnp.arange(LEN, dtype=jnp.int32)
    visible = positions[None, None, :] <= positions[:, None, None]
    scores = jnp.where(visible, scores, MASK_VALUE)
    row_max = lax.optimization_barrier(jnp.max(scores, axis=-1, keepdims=True))
    weights = jnp.where(visible, jnp.exp(scores - row_max), 0.0)
    totals = lax.optimization_barrier(jnp.sum(weights, axis=-1))
    mixture = jnp.einsum('phj,ja->pha', weights.astype(jnp.bfloat16).astype(jnp.float32), key_lat.astype(jnp.float32))
    return (mixture / totals[..., None]).astype(jnp.bfloat16)

def decode_group(inputs):
    query_lat, query_pos, key_lat, key_pos, own_lat, own_pos = inputs
    query_lat = query_lat.astype(jnp.float32)
    query_pos = query_pos.reshape(SAMPLES, STEPS, HEADS, ROPE).astype(jnp.float32)
    far_scores = jnp.einsum('stha,ja->sthj', query_lat, key_lat.astype(jnp.float32))
    far_scores = (far_scores + jnp.einsum('sthb,jb->sthj', query_pos, key_pos.astype(jnp.float32))) * SOFTMAX_SCALE
    near_scores = jnp.einsum('stha,sua->sthu', query_lat, own_lat.astype(jnp.float32))
    near_scores = (near_scores + jnp.einsum('sthb,sub->sthu', query_pos, own_pos.astype(jnp.float32))) * SOFTMAX_SCALE
    step_ids = jnp.arange(STEPS, dtype=jnp.int32)
    visible = (step_ids[None, :] <= step_ids[:, None])[None, :, None, :]
    near_scores = jnp.where(visible, near_scores, MASK_VALUE)
    row_max = jnp.maximum(lax.optimization_barrier(jnp.max(far_scores, axis=-1)), lax.optimization_barrier(jnp.max(near_scores, axis=-1)))[..., None]
    far_weights = jnp.exp(far_scores - row_max)
    near_weights = jnp.where(visible, jnp.exp(near_scores - row_max), 0.0)
    totals = lax.optimization_barrier(jnp.sum(far_weights, axis=-1)) + lax.optimization_barrier(jnp.sum(near_weights, axis=-1))
    mixture = jnp.einsum('sthj,ja->stha', far_weights.astype(jnp.bfloat16).astype(jnp.float32), key_lat.astype(jnp.float32))
    mixture = mixture + jnp.einsum('sthu,sua->stha', near_weights.astype(jnp.bfloat16).astype(jnp.float32), own_lat.astype(jnp.float32))
    return (mixture / totals[..., None]).astype(jnp.bfloat16)

def reference(prompt_query, prompt_query_pos, prompt_latent, prompt_pos, decode_query, decode_query_pos, decode_latent, decode_pos, decode_hidden, norm_gain, value_up, out_proj, route_ids, route_gates, expert_gate, expert_up, expert_down):
    prefill_out = lax.map(prefill_group, (prompt_query, prompt_query_pos, prompt_latent, prompt_pos))
    decode_mix = lax.map(decode_group, (decode_query, decode_query_pos, prompt_latent, prompt_pos, decode_latent, decode_pos))
    tokens = GROUPS * SAMPLES * STEPS
    head_values = jnp.einsum('nha,hav->nhv', decode_mix.reshape(tokens, HEADS, LAT).astype(jnp.float32), value_up.astype(jnp.float32)).astype(jnp.bfloat16)
    attention = jnp.dot(head_values.reshape(tokens, HEADS * HV), out_proj, preferred_element_type=jnp.float32)
    hidden_sum = decode_hidden.reshape(tokens, D).astype(jnp.float32) + attention
    scale_rows = lax.rsqrt(lax.optimization_barrier(jnp.mean(hidden_sum * hidden_sum, axis=-1, keepdims=True)) + NORM_EPS)
    normed = (hidden_sum * scale_rows * norm_gain.astype(jnp.float32)).astype(jnp.bfloat16)
    gate_values = route_gates.reshape(tokens, TOPK).astype(jnp.float32)
    route_weights = ROUTE_SCALE * gate_values / lax.optimization_barrier(jnp.sum(gate_values, axis=-1, keepdims=True))
    chosen = route_ids.reshape(tokens, TOPK)

    def one_expert(running, items):
        expert_id, w_gate, w_up, w_down = items
        gate_act = jnp.dot(normed, w_gate, preferred_element_type=jnp.float32)
        up_act = jnp.dot(normed, w_up, preferred_element_type=jnp.float32)
        expert_hidden = (jax.nn.silu(gate_act) * up_act).astype(jnp.bfloat16)
        result = jnp.dot(expert_hidden, w_down, preferred_element_type=jnp.float32)
        shares = lax.optimization_barrier(jnp.sum(jnp.where(chosen == expert_id, route_weights, 0.0), axis=-1))
        return (running + shares[:, None] * result, None)
    routed, _ = lax.scan(one_expert, jnp.zeros((tokens, D), jnp.float32), (jnp.arange(EXPERTS, dtype=jnp.int32), expert_gate, expert_up, expert_down))
    decode_out = (hidden_sum + routed).astype(jnp.bfloat16).reshape(GROUPS, SAMPLES, STEPS, D)
    return (prefill_out, decode_out)
```

```python
import functools

import jax
import jax.numpy as jnp
from jax import lax
from jax.experimental import pallas as pl
from jax.experimental.pallas import tpu as pltpu
from jax.sharding import PartitionSpec as P

SOFTMAX_SCALE = 192.0 ** (-0.5)
MASK_VALUE = -1e30
NORM_EPS = 1e-06
ROUTE_SCALE = 2.5

CTX, EP = 16, 16
BOTH = ("ctx", "ep")
BF16, F32 = jnp.bfloat16, jnp.float32

HOPS = {
    "xa": ("x", 1),
    "xb": ("x", 3),
    "ya": ("y", 1),
    "yb": ("y", 3),
    "z1": ("z_lo", 1),
    "z2": ("z_lo", 2),
    "zh": ("z_hi", 1),
    "core": ("core", 1),
}
GRAY = (0, 1, 3, 2)
CYCLE = ("xa", "ya", "xb", "yb")
EXTRA = 128
CHUNK = 8


def place_of(device):
    ctx, ep = divmod(device, EP)
    return {"z_hi": ctx // 8, "y": ctx // 2 % 4, "core": ctx % 2, "z_lo": ep // 4, "x": ep % 4}


def device_at(place):
    ctx = (place["z_hi"] * 4 + place["y"]) * 2 + place["core"]
    return ctx * EP + place["z_lo"] * 4 + place["x"]


@functools.cache
def pairs_of(hop, other_hop):
    pairs = []
    for device in range(CTX * EP):
        place = place_of(device)
        axis, flip = HOPS[hop if place["core"] == 0 else other_hop]
        place[axis] ^= flip
        pairs.append((device, device_at(place)))
    return tuple(pairs)


def swap(array, hop, other_hop=None):
    return lax.ppermute(array, BOTH, pairs_of(hop, other_hop or hop))


def dot(a, b):
    return jnp.dot(a, b, preferred_element_type=F32)


def nt_dot(a, b):
    return lax.dot_general(a, b, (((1,), (1,)), ((), ())), preferred_element_type=F32)


def prefill_body(query_ref, query_pos_ref, keys_ref, bias_ref, *rest):
    out_ref = rest[-1]
    positions, heads, lat = query_ref.shape
    rope = query_pos_ref.shape[-1]
    step = 4
    key_lat = keys_ref[:, :lat]
    key_pos = keys_ref[:, lat : lat + rope]
    for start in range(0, positions, step):
        part = pl.ds(start, step)
        scores = nt_dot(query_ref[part].reshape(step * heads, lat), key_lat)
        scores += nt_dot(query_pos_ref[part].reshape(step * heads, rope), key_pos)
        bias = jnp.broadcast_to(bias_ref[part][:, None, :], (step, heads, keys_ref.shape[0]))
        scores = scores * SOFTMAX_SCALE + bias.reshape(scores.shape)
        weights = jnp.exp(scores - jnp.max(scores, axis=-1, keepdims=True))
        totals = jnp.sum(weights, axis=-1, keepdims=True)
        mix = dot(weights.astype(BF16), key_lat) / totals
        out_ref[part] = mix.astype(BF16).reshape(step, heads, lat)


def prefill_chunk(index, query, query_pos, keys, bias, running):
    rows, heads, lat = query.shape
    rope = query_pos.shape[-1]
    cube = pl.BlockSpec((CHUNK, heads, lat), lambda i: (index, 0, 0))
    in_specs = [
        cube,
        pl.BlockSpec((CHUNK, heads, rope), lambda i: (index, 0, 0)),
        pl.BlockSpec(keys.shape, lambda i: (0, 0)),
        pl.BlockSpec((CHUNK, bias.shape[1]), lambda i: (index, 0)),
    ]
    operands = [query, query_pos, keys, bias]
    aliases = {}
    if running is not None:
        in_specs.append(pl.BlockSpec(memory_space=pl.ANY))
        operands.append(running)
        aliases = {4: 0}
    work = CHUNK * heads * keys.shape[0]
    return pl.pallas_call(
        prefill_body,
        out_shape=jax.ShapeDtypeStruct((rows, heads, lat), BF16),
        grid=(1,),
        in_specs=in_specs,
        out_specs=cube,
        input_output_aliases=aliases,
        compiler_params=pltpu.CompilerParams(vmem_limit_bytes=32 * 2**20),
        cost_estimate=pl.CostEstimate(
            flops=2 * work * (2 * lat + rope), bytes_accessed=4 * CHUNK * heads * lat, transcendentals=work
        ),
        name="prefill_chunk",
    )(*operands)


def decode_body(core_ref, query_ref, keys_ref, own_ref, up_ref, proj_ref, inject_ref, keep_ref, send_ref):
    heads, lat, width = up_ref.shape
    tokens = own_ref.shape[0]
    rows = heads * tokens
    query = query_ref[...]
    far = nt_dot(query, keys_ref[...]) * SOFTMAX_SCALE
    near = nt_dot(query, own_ref[...]) * SOFTMAX_SCALE
    token = lax.broadcasted_iota(jnp.int32, (rows, tokens), 0) % tokens
    key = lax.broadcasted_iota(jnp.int32, (rows, tokens), 1)
    visible = (token // 2 == key // 2) & (key <= token)
    near = jnp.where(visible, near, MASK_VALUE)
    top = jnp.maximum(jnp.max(far, axis=-1, keepdims=True), jnp.max(near, axis=-1, keepdims=True))
    far = jnp.exp(far - top)
    near = jnp.where(visible, jnp.exp(near - top), 0.0)
    totals = jnp.sum(far, axis=-1, keepdims=True) + jnp.sum(near, axis=-1, keepdims=True)
    mix = dot(far.astype(BF16), keys_ref[:, :lat]) + dot(near.astype(BF16), own_ref[:, :lat])
    mix = (mix / totals).astype(BF16)
    values = [dot(mix[h * tokens : (h + 1) * tokens], up_ref[h]).astype(BF16) for h in range(heads)]
    values = jnp.concatenate(values, axis=1)
    half = proj_ref.shape[1] // 2
    low, high = dot(values, proj_ref[:, :half]), dot(values, proj_ref[:, half:])
    first = core_ref[0] == 0
    mine, other = jnp.where(first, low, high), jnp.where(first, high, low)
    own_rows = inject_ref.shape[1]
    pad = jnp.zeros((tokens - own_rows, EXTRA), F32)
    for ref, values, at in ((keep_ref, mine, 0), (send_ref, other, 1)):
        add = inject_ref[at]
        ref[:, :EXTRA] = jnp.concatenate([add[:, :EXTRA], pad], axis=0).astype(ref.dtype)
        ref[:own_rows, EXTRA:] = (values[:own_rows] + add[:, EXTRA:]).astype(ref.dtype)
        ref[own_rows:, EXTRA:] = values[own_rows:].astype(ref.dtype)


def decode_attention(core, query, keys, own, up, proj, inject):
    tokens, half = own.shape[0], proj.shape[1] // 2
    vmem = pl.BlockSpec(memory_space=pltpu.VMEM)
    return pl.pallas_call(
        decode_body,
        out_shape=(
            jax.ShapeDtypeStruct((tokens, EXTRA + half), F32),
            jax.ShapeDtypeStruct((tokens, EXTRA + half), BF16),
        ),
        in_specs=[pl.BlockSpec(memory_space=pltpu.SMEM)] + [vmem] * 6,
        out_specs=(vmem, vmem),
        compiler_params=pltpu.CompilerParams(vmem_limit_bytes=32 * 2**20),
        cost_estimate=pl.CostEstimate(flops=10**9, bytes_accessed=6 * 10**6, transcendentals=10**5),
        name="decode_attention",
    )(core.reshape(1), query, keys, own, up, proj, inject)


def pick(core, pieces):
    first = core == 0
    return jnp.where(first, pieces[0], pieces[1]), jnp.where(first, pieces[1], pieces[0])


def gather_keys(block):
    far = swap(block, "zh")
    near_a, far_a = swap(block, "ya", "yb"), swap(far, "yb", "ya")
    near, far = jnp.concatenate([block, near_a]), jnp.concatenate([far, far_a])
    near_b, far_b = swap(near, "yb", "ya"), swap(far, "ya", "yb")
    half = jnp.concatenate([near, near_b, far, far_b])
    return jnp.concatenate([half, swap(half, "core")])


def slot_blocks(z_hi, y, core):
    orders = jnp.array([[0, 1, 3, 2], [0, 3, 1, 2]], jnp.int32)
    blocks = []
    for flip in (0, 1):
        side = core ^ flip
        for z_flip in (0, 1):
            blocks.append(((z_hi ^ z_flip) * 4 + (y ^ orders[side ^ z_flip])) * 2 + side)
    return jnp.concatenate(blocks)


def on_device(
    prompt_query,
    prompt_query_pos,
    prompt_latent,
    prompt_pos,
    decode_query,
    decode_query_pos,
    decode_latent,
    decode_pos,
    decode_hidden,
    norm_gain,
    value_up,
    out_proj,
    route_ids,
    route_gates,
    expert_gate,
    expert_up,
    expert_down,
):
    ctx = lax.axis_index("ctx")
    z_hi, y, core = ctx // 8, ctx // 2 % 4, ctx % 2
    expert = lax.axis_index("ep")
    query = prompt_query[0]
    positions, heads, lat = query.shape
    rope = prompt_pos.shape[-1]
    width = decode_hidden.shape[-1]
    half = width // 2
    steps = decode_hidden.shape[2]
    own_heads = value_up.shape[0]

    pad = jnp.zeros((positions, EXTRA - rope), BF16)
    block = jnp.concatenate([prompt_latent[0], prompt_pos[0], pad], axis=1)
    lat_part = decode_query[0, 0].reshape(steps, CTX, own_heads, lat)
    pos_part = decode_query_pos[0, 0].reshape(steps, CTX, own_heads, rope)
    queries = jnp.concatenate(
        [lat_part, pos_part, jnp.zeros((steps, CTX, own_heads, EXTRA - rope), BF16)], axis=-1
    )
    queries = queries.transpose(1, 2, 0, 3).reshape(CTX, own_heads * steps, -1)
    own = jnp.concatenate([decode_latent[0, 0], decode_pos[0, 0], pad[:steps]], axis=1)
    own = jnp.broadcast_to(own[None], (CTX, steps, own.shape[1]))
    sent = jnp.concatenate([queries, own], axis=1)
    got = lax.all_to_all(sent, "ctx", split_axis=0, concat_axis=0, tiled=True)
    slots = jnp.arange(CTX, dtype=jnp.int32)
    gray = jnp.array(GRAY, jnp.int32)[slots // 2 % 4]
    order = ((z_hi ^ (slots // 8)) * 4 + (y ^ gray)) * 2 + slots % 2
    sorting = (order[:, None] == slots[None, :]).astype(BF16)
    got = jnp.einsum("ij,jrc->irc", sorting, got, preferred_element_type=F32).astype(BF16)
    queries = got[:, : own_heads * steps].reshape(CTX, own_heads, steps, -1)
    queries = queries.transpose(1, 0, 2, 3).reshape(own_heads * CTX * steps, -1)
    own = got[:, own_heads * steps :].reshape(CTX * steps, -1)

    hidden = decode_hidden[0, 0].astype(F32)
    routes = jnp.concatenate(
        [
            route_ids[0, 0].astype(F32),
            route_gates[0, 0].astype(F32),
            jnp.zeros((steps, EXTRA - 2 * route_ids.shape[-1]), F32),
        ],
        axis=1,
    )
    row_core = jnp.arange(8, dtype=jnp.int32)[:, None] // steps
    injected = []
    for part in pick(core, (hidden[:, :half], hidden[:, half:])):
        rows = jnp.tile(jnp.concatenate([routes, part], axis=1), (8 // steps, 1))
        injected.append(jnp.where(row_core == core, rows, 0.0))
    inject = jnp.stack(injected)

    both = jnp.concatenate([expert_gate[0], expert_up[0]], axis=1)
    mine, other = pick(core, (both[:half], both[half:]))
    weight_in = jnp.concatenate([mine, swap(other, "core")], axis=1)
    down = lax.all_to_all(expert_down[0], "ctx", split_axis=0, concat_axis=1, tiled=True)
    mine, other = pick(core, (down[:, :half], down[:, half:]))
    weight_out = jnp.concatenate([mine, swap(other, "core")], axis=0)

    keys = gather_keys(block)

    key_rows = (slot_blocks(z_hi, y, core)[:, None] * positions + jnp.arange(positions)[None]).reshape(-1)
    query_rows = ctx * positions + jnp.arange(positions)
    bias = jnp.where(key_rows[None, :] <= query_rows[:, None], 0.0, MASK_VALUE).astype(F32)
    query_pos = prompt_query_pos[0].reshape(positions, heads, rope)
    state = {"next": 0, "out": None}

    def chunk_beside(start, result):
        index = state["next"]
        if index * CHUNK >= positions:
            return result
        tied, start = lax.optimization_barrier((bias, start))
        state["out"] = prefill_chunk(index, query, query_pos, keys, tied, state["out"])
        state["next"] = index + 1
        result, state["out"] = lax.optimization_barrier((result, state["out"]))
        return result

    def exchange(array, hop, other_hop=None, beside=True):
        result = swap(array, hop, other_hop)
        return chunk_beside(array, result) if beside else result

    keep, send = decode_attention(core, queries, keys, own, value_up, out_proj, inject)
    summed = keep + swap(send, "core").astype(F32)
    summed = summed.reshape(2, 4, 2 * steps, -1)
    part = exchange(summed[:, 2:].astype(BF16), "yb")
    summed = summed[:, :2] + part.astype(F32)
    part = exchange(summed[:, 1].astype(BF16), "ya")
    summed = summed[:, 0] + part.astype(F32)
    part = exchange(summed.astype(BF16), "zh")
    summed = summed + part[::-1].astype(F32)
    summed = summed.reshape(4 * steps, -1)
    hidden_sum = summed[:, EXTRA:]
    squares = jnp.sum(hidden_sum * hidden_sum, axis=-1, keepdims=True)
    squares = squares + swap(jnp.broadcast_to(squares, (4 * steps, EXTRA)), "core")[:, :1]
    gain, _ = pick(core, (norm_gain[:half], norm_gain[half:]))
    scale_rows = lax.rsqrt(squares / width + NORM_EPS)
    normed = hidden_sum * scale_rows * gain.astype(F32)
    tokens = jnp.concatenate([summed[:, :EXTRA], normed], axis=1).astype(BF16)

    tokens = jnp.concatenate([tokens, exchange(tokens, "z1")])
    tokens = jnp.concatenate([tokens, exchange(tokens, "z2")])
    rows = tokens.shape[0]
    quarter = half // 2
    lanes = [tokens[:, : EXTRA + quarter], tokens[:, EXTRA + quarter :]]
    for step in range(4):
        moved = [swap(lane, CYCLE[(n + step) % 4], CYCLE[(n + step + 2) % 4]) for n, lane in enumerate(lanes)]
        moved[0] = chunk_beside(lanes[0], moved[0])
        lanes = [jnp.concatenate(pair) for pair in zip(lanes, moved)]

    def turn(array, axes):
        cube = array.reshape((2, 2, 2, 2, rows, array.shape[-1]))
        return cube.transpose(axes + (4, 5)).reshape(array.shape)

    routes = lanes[0][:, :EXTRA].astype(F32)
    choices = route_ids.shape[-1]
    ids, gates = routes[:, :choices], routes[:, choices : 2 * choices]
    named = jnp.where(ids == expert.astype(F32), gates, 0.0)
    shares = ROUTE_SCALE * jnp.sum(named, axis=-1, keepdims=True) / jnp.sum(gates, axis=-1, keepdims=True)
    acts = dot(lanes[0][:, EXTRA:], weight_in[:quarter])
    acts += turn(dot(lanes[1], weight_in[quarter:]), (1, 2, 3, 0))
    units = expert_gate.shape[-1]
    other = turn(acts[:, 2 * units :].astype(BF16), (2, 3, 0, 1))
    acts = acts[:, : 2 * units] + swap(other, "core").astype(F32)
    expert_hidden = (jax.nn.silu(acts[:, :units]) * acts[:, units:]).astype(BF16)
    other = turn(expert_hidden, (2, 3, 0, 1))
    expert_hidden = jnp.concatenate([expert_hidden, swap(other, "core")], axis=1)

    results = []
    for n in range(2):
        rows_in, scales = expert_hidden, shares
        if n == 1:
            rows_in, scales = turn(rows_in, (3, 0, 1, 2)), turn(scales, (3, 0, 1, 2))
        weights = weight_out[:, n * quarter : (n + 1) * quarter]
        middle = rows_in.shape[0] // 2
        results.append([rows_in, scales, weights, middle])
    lanes = []
    for rows_in, scales, weights, middle in results:
        lanes.append((dot(rows_in[middle:], weights) * scales[middle:]).astype(BF16))
    moved = [swap(lane, CYCLE[(n + 3) % 4], CYCLE[(n + 5) % 4]) for n, lane in enumerate(lanes)]
    lanes = []
    for (rows_in, scales, weights, middle), part in zip(results, moved):
        lanes.append(dot(rows_in[:middle], weights) * scales[:middle] + part.astype(F32))
    for step in (2, 1, 0):
        middle = lanes[0].shape[0] // 2
        moved = [
            swap(lane[middle:].astype(BF16), CYCLE[(n + step) % 4], CYCLE[(n + step + 2) % 4])
            for n, lane in enumerate(lanes)
        ]
        lanes = [lane[:middle] + part.astype(F32) for lane, part in zip(lanes, moved)]
    routed = jnp.concatenate(lanes, axis=1)
    for hop in ("z2", "z1", "zh"):
        middle = routed.shape[0] // 2
        routed = routed[:middle] + swap(routed[middle:].astype(BF16), hop).astype(F32)
    final = (hidden_sum[: 2 * steps] + routed).astype(BF16)
    mine, other = pick(core, (final[:steps], final[steps:]))
    other = swap(other, "core")
    left, right = pick(core, (mine, other))
    decode_out = jnp.concatenate([left, right], axis=1)[None, None]
    while state["next"] * CHUNK < positions:
        decode_out = chunk_beside(bias, decode_out)
    return (state["out"][None], decode_out)


def solution(mesh):
    in_specs = (
        P("ep", "ctx", None, None),
        P("ep", "ctx", None),
        P("ep", "ctx", None),
        P("ep", "ctx", None),
        P("ep", "ctx", None, None, None),
        P("ep", "ctx", None, None),
        P("ep", "ctx", None, None),
        P("ep", "ctx", None, None),
        P("ep", "ctx", None, None),
        P(),
        P("ctx", None, None),
        P("ctx", None),
        P("ep", "ctx", None, None),
        P("ep", "ctx", None, None),
        P("ep", None, "ctx"),
        P("ep", None, "ctx"),
        P("ep", None, "ctx"),
    )
    out_specs = (P("ep", "ctx", None, None), P("ep", "ctx", None, None))
    return jax.shard_map(
        on_device, mesh=mesh, in_specs=in_specs, out_specs=out_specs, check_vma=False
    )
```

```python
import functools

import jax
import jax.numpy as jnp
from jax import lax
from jax.experimental import pallas as pl
from jax.experimental.pallas import tpu as pltpu
from jax.sharding import PartitionSpec as P

SOFTMAX_SCALE = 192.0 ** (-0.5)
MASK_VALUE = -1e30
NORM_EPS = 1e-06
ROUTE_SCALE = 2.5

CTX, EP = 16, 16
BOTH = ("ctx", "ep")
BF16, F32 = jnp.bfloat16, jnp.float32

HOPS = {
    "xa": ("x", 1),
    "xb": ("x", 3),
    "ya": ("y", 1),
    "yb": ("y", 3),
    "z1": ("z_lo", 1),
    "z2": ("z_lo", 2),
    "zh": ("z_hi", 1),
    "core": ("core", 1),
}
GRAY = (0, 1, 3, 2)
EXTRA = 128
CHUNK = 8
SMALL_HOPS = (("xa", "xb"), ("ya", "yb"))
Y_HOPS = (("ya", "ya"), ("yb", "yb"))
Z_HOPS = (("z1", "z1"), ("z2", "z2"))
LARGE_HOPS = ((("xb", "xa"), ("yb", "ya")), (("yb", "ya"), ("xb", "xa")))
PREFILL_AT = {"sum": 0, "gather": (0, 1), "back": (2, 2, 2, 1, 0)}


def place_of(device):
    ctx, ep = divmod(device, EP)
    return {"z_hi": ctx // 8, "y": ctx // 2 % 4, "core": ctx % 2, "z_lo": ep // 4, "x": ep % 4}


def device_at(place):
    ctx = (place["z_hi"] * 4 + place["y"]) * 2 + place["core"]
    return ctx * EP + place["z_lo"] * 4 + place["x"]


@functools.cache
def pairs_of(hop, other_hop):
    pairs = []
    for device in range(CTX * EP):
        place = place_of(device)
        for name in (hop if place["core"] == 0 else other_hop).split("+"):
            axis, flip = HOPS[name]
            place[axis] ^= flip
        pairs.append((device, device_at(place)))
    return tuple(pairs)


def swap(array, hop, other_hop=None):
    return lax.ppermute(array, BOTH, pairs_of(hop, other_hop or hop))


def swap_square(blocks, hops):
    both = tuple("+".join(pair) for pair in zip(*hops))
    return [swap(block, *hop) for block, hop in zip(blocks, (*hops, both))]


def dot(a, b):
    return jnp.dot(a, b, preferred_element_type=F32)


def nt_dot(a, b):
    return lax.dot_general(a, b, (((1,), (1,)), ((), ())), preferred_element_type=F32)


def prefill_body(query_ref, query_pos_ref, near_ref, far_ref, bias_ref, *rest):
    out_ref = rest[-1]
    positions, heads, lat = query_ref.shape
    rope = query_pos_ref.shape[-1]
    step = 4
    sides = (near_ref, far_ref)
    count = near_ref.shape[0]
    for start in range(0, positions, step):
        part = pl.ds(start, step)
        lat_rows = query_ref[part].reshape(step * heads, lat)
        pos_rows = query_pos_ref[part].reshape(step * heads, rope)
        scores = []
        for side, ref in enumerate(sides):
            score = nt_dot(lat_rows, ref[:, :lat]) + nt_dot(pos_rows, ref[:, lat : lat + rope])
            bias = bias_ref[part, side * count : (side + 1) * count]
            bias = jnp.broadcast_to(bias[:, None, :], (step, heads, count)).reshape(score.shape)
            scores.append(score * SOFTMAX_SCALE + bias)
        top = jnp.maximum(*[jnp.max(score, axis=-1, keepdims=True) for score in scores])
        weights = [jnp.exp(score - top) for score in scores]
        totals = sum(jnp.sum(weight, axis=-1, keepdims=True) for weight in weights)
        mix = sum(dot(weight.astype(BF16), ref[:, :lat]) for weight, ref in zip(weights, sides))
        out_ref[part] = (mix / totals).astype(BF16).reshape(step, heads, lat)


def prefill_block(index, query, query_pos, keys, bias, running):
    rows, heads, lat = query.shape
    cube = pl.BlockSpec((CHUNK, heads, lat), lambda i: (index, 0, 0))
    in_specs = [cube, pl.BlockSpec((CHUNK, heads, query_pos.shape[2]), lambda i: (index, 0, 0))]
    in_specs += [pl.BlockSpec(key.shape, lambda i: (0, 0)) for key in keys]
    in_specs.append(pl.BlockSpec((CHUNK, bias.shape[1]), lambda i: (index, 0)))
    operands = [query, query_pos, *keys, bias]
    aliases = {}
    if running is not None:
        in_specs.append(pl.BlockSpec(memory_space=pl.ANY))
        operands.append(running)
        aliases = {5: 0}
    work = CHUNK * heads * bias.shape[1]
    return pl.pallas_call(
        prefill_body,
        out_shape=jax.ShapeDtypeStruct((rows, heads, lat), BF16),
        grid=(1,),
        in_specs=in_specs,
        out_specs=cube,
        input_output_aliases=aliases,
        compiler_params=pltpu.CompilerParams(vmem_limit_bytes=32 * 2**20),
        cost_estimate=pl.CostEstimate(
            flops=2 * work * (2 * lat + query_pos.shape[2]), bytes_accessed=4 * CHUNK * heads * lat, transcendentals=work
        ),
        name="prefill_block",
    )(*operands)


def decode_body(
    core_ref, query_ref, near_ref, far_ref, own_ref, inject_ref, up_any, proj_any, keep_ref, send_ref, up_ref, proj_ref, sems
):
    up_copy = pltpu.make_async_copy(up_any, up_ref, sems.at[0])
    proj_copy = pltpu.make_async_copy(proj_any, proj_ref, sems.at[1])
    up_copy.start()
    proj_copy.start()
    heads, lat, width = up_ref.shape
    tokens = own_ref.shape[0]
    rows = heads * tokens
    query = query_ref[...]
    sides = (near_ref, far_ref)
    far = [nt_dot(query, ref[...]) * SOFTMAX_SCALE for ref in sides]
    near = nt_dot(query, own_ref[...]) * SOFTMAX_SCALE
    token = lax.broadcasted_iota(jnp.int32, (rows, tokens), 0) % tokens
    key = lax.broadcasted_iota(jnp.int32, (rows, tokens), 1)
    visible = (token // 2 == key // 2) & (key <= token)
    near = jnp.where(visible, near, MASK_VALUE)
    top = jnp.max(near, axis=-1, keepdims=True)
    for part in far:
        top = jnp.maximum(top, jnp.max(part, axis=-1, keepdims=True))
    near = jnp.where(visible, jnp.exp(near - top), 0.0)
    totals = jnp.sum(near, axis=-1, keepdims=True)
    mix = dot(near.astype(BF16), own_ref[:, :lat])
    for part, ref in zip(far, sides):
        weights = jnp.exp(part - top)
        totals += jnp.sum(weights, axis=-1, keepdims=True)
        mix += dot(weights.astype(BF16), ref[:, :lat])
    mix = (mix / totals).astype(BF16)
    up_copy.wait()
    values = [dot(mix[h * tokens : (h + 1) * tokens], up_ref[h]).astype(BF16) for h in range(heads)]
    values = jnp.concatenate(values, axis=1)
    proj_copy.wait()
    half = proj_ref.shape[1] // 2
    low, high = dot(values, proj_ref[:, :half]), dot(values, proj_ref[:, half:])
    first = core_ref[0] == 0
    mine, other = jnp.where(first, low, high), jnp.where(first, high, low)
    own_rows = inject_ref.shape[1]
    pad = jnp.zeros((tokens - own_rows, EXTRA), F32)
    for ref, values, at in ((keep_ref, mine, 0), (send_ref, other, 1)):
        add = inject_ref[at]
        ref[:, :EXTRA] = jnp.concatenate([add[:, :EXTRA], pad], axis=0).astype(ref.dtype)
        ref[:own_rows, EXTRA:] = (values[:own_rows] + add[:, EXTRA:]).astype(ref.dtype)
        ref[own_rows:, EXTRA:] = values[own_rows:].astype(ref.dtype)


def decode_attention(core, query, keys, own, inject, up, proj):
    tokens, half = own.shape[0], proj.shape[1] // 2
    vmem = pl.BlockSpec(memory_space=pltpu.VMEM)
    return pl.pallas_call(
        decode_body,
        out_shape=(
            jax.ShapeDtypeStruct((tokens, EXTRA + half), F32),
            jax.ShapeDtypeStruct((tokens, EXTRA + half), BF16),
        ),
        in_specs=[pl.BlockSpec(memory_space=pltpu.SMEM)] + [vmem] * 5 + [pl.BlockSpec(memory_space=pl.ANY)] * 2,
        out_specs=(vmem, vmem),
        scratch_shapes=[
            pltpu.VMEM(up.shape, BF16),
            pltpu.VMEM(proj.shape, BF16),
            pltpu.SemaphoreType.DMA((2,)),
        ],
        compiler_params=pltpu.CompilerParams(vmem_limit_bytes=40 * 2**20),
        cost_estimate=pl.CostEstimate(flops=10**9, bytes_accessed=6 * 10**6, transcendentals=10**5),
        name="decode_attention",
    )(core.reshape(1), query, *keys, own, inject, up, proj)


def after(value, *others):
    return lax.optimization_barrier((value, *others))[1:]


LANE_BLOCK = [b // 4 % 2 * 8 + b // 8 * 4 + b % 4 for b in range(16)]
CORE_BLOCK = [b % 4 * 4 + b // 4 for b in range(16)]


def add_lanes(lane_refs, low, high, part_ref, out_ref, blocks):
    near0, far0, near1, far1 = lane_refs
    middle = near0.shape[0]
    rows = middle // 8
    for ref, at in ((near1, 0), (far1, middle)):
        part_ref[pl.ds(at, middle)] = dot(ref[...], high)
    for ref, first in ((near0, 0), (far0, 8)):
        acts = dot(ref[:, EXTRA:], low)
        for n in range(8):
            b = first + n
            block = acts[n * rows : (n + 1) * rows] + part_ref[pl.ds(LANE_BLOCK[b] * rows, rows)]
            out_ref[pl.ds(blocks[b] * rows, rows)] = block.astype(out_ref.dtype)


def other_acts_body(*refs):
    lane_refs, (got_ref, out_ref, part_ref) = refs[:4], refs[4:]
    quarter = lane_refs[2].shape[1]
    add_lanes(lane_refs, got_ref[:quarter], got_ref[quarter:], part_ref, out_ref, CORE_BLOCK)


def own_acts_body(place_ref, *refs):
    lane_refs, (gate_ref, up_ref, out_ref, shares_ref, part_ref) = refs[:4], refs[4:]
    middle, quarter = lane_refs[2].shape
    base = pl.multiple_of(place_ref[0] * (2 * quarter), 2 * quarter)
    for ref, at in zip(lane_refs[:2], (0, middle)):
        gates = ref[:, :EXTRA].astype(F32)
        here = lax.broadcasted_iota(jnp.int32, gates.shape, 1) == place_ref[1]
        gate = jnp.sum(jnp.where(here, gates, 0.0), axis=1, keepdims=True)
        share = ROUTE_SCALE * gate / jnp.sum(gates, axis=1, keepdims=True)
        shares_ref[pl.ds(at, middle)] = jnp.broadcast_to(share, gates.shape)
    sides = []
    for start in (0, quarter):
        part = pl.ds(base + start, quarter)
        sides.append(jnp.concatenate([gate_ref[part], up_ref[part]], axis=1))
    add_lanes(lane_refs, *sides, part_ref, out_ref, range(16))


def expert_acts(body, kinds, width, scalars, arrays):
    count = 2 * arrays[0].shape[0]
    vmem, smem = (pl.BlockSpec(memory_space=space) for space in (pltpu.VMEM, pltpu.SMEM))
    return pl.pallas_call(
        body,
        out_shape=[jax.ShapeDtypeStruct((count, size), kind) for size, kind in zip((width, EXTRA), kinds)],
        in_specs=[smem] * len(scalars) + [vmem] * len(arrays),
        out_specs=[vmem] * len(kinds),
        scratch_shapes=[pltpu.VMEM((count, width), F32)],
        compiler_params=pltpu.CompilerParams(vmem_limit_bytes=24 * 2**20),
        cost_estimate=pl.CostEstimate(flops=5 * 10**8, bytes_accessed=3 * 10**6, transcendentals=0),
        name="expert_acts",
    )(*scalars, *arrays)


def results_body(lane, place_ref, hidden_ref, other_ref, down_ref, got_ref, shares_ref, send_ref, keep_ref):
    chunks, depth, units = got_ref.shape
    part = slice(lane * chunks // 2, (lane + 1) * chunks // 2)
    mine = down_ref[pl.ds(place_ref[0] * chunks + part.start, chunks // 2)].reshape(-1, units)
    theirs = got_ref[part].reshape(-1, units)
    count = hidden_ref.shape[0]
    rows, middle = count // 16, count // 2
    result = nt_dot(hidden_ref[...], mine) + nt_dot(other_ref[...], theirs)
    result = result * jnp.concatenate([shares_ref[...]] * (result.shape[1] // EXTRA), axis=1)
    for b in range(16):
        at = (LANE_BLOCK[b] if lane else b) * rows
        block = result[b * rows : (b + 1) * rows]
        if at < middle:
            keep_ref[pl.ds(at, rows)] = block
        else:
            send_ref[pl.ds(at - middle, rows)] = block.astype(BF16)


def expert_results(lane, place, hidden, other, down, got, shares):
    shape = (hidden.shape[0] // 2, got.shape[0] // 2 * got.shape[1])
    vmem = pl.BlockSpec(memory_space=pltpu.VMEM)
    return pl.pallas_call(
        functools.partial(results_body, lane),
        out_shape=(jax.ShapeDtypeStruct(shape, BF16), jax.ShapeDtypeStruct(shape, F32)),
        in_specs=[pl.BlockSpec(memory_space=pltpu.SMEM)] + [vmem] * 5,
        out_specs=(vmem, vmem),
        compiler_params=pltpu.CompilerParams(vmem_limit_bytes=24 * 2**20),
        cost_estimate=pl.CostEstimate(flops=5 * 10**8, bytes_accessed=3 * 10**6, transcendentals=0),
        name="expert_results",
    )(place, hidden, other, down, got, shares)


def pick(core, pieces):
    first = core == 0
    return jnp.where(first, pieces[0], pieces[1]), jnp.where(first, pieces[1], pieces[0])


def slot_blocks(z_hi, y, core):
    orders = jnp.array([[0, 1, 3, 2], [0, 3, 1, 2]], jnp.int32)
    blocks = []
    for flip in (0, 1):
        side = core ^ flip
        for z_flip in (0, 1):
            blocks.append(((z_hi ^ z_flip) * 4 + (y ^ orders[side ^ z_flip])) * 2 + side)
    return jnp.concatenate(blocks)


def on_device(
    prompt_query,
    prompt_query_pos,
    prompt_latent,
    prompt_pos,
    decode_query,
    decode_query_pos,
    decode_latent,
    decode_pos,
    decode_hidden,
    norm_gain,
    value_up,
    out_proj,
    route_ids,
    route_gates,
    expert_gate,
    expert_up,
    expert_down,
):
    ctx = lax.axis_index("ctx")
    z_hi, y, core = ctx // 8, ctx // 2 % 4, ctx % 2
    expert = lax.axis_index("ep")
    query = prompt_query[0]
    positions, heads, lat = query.shape
    rope = prompt_pos.shape[-1]
    width = decode_hidden.shape[-1]
    half = width // 2
    steps = decode_hidden.shape[2]
    own_heads = value_up.shape[0]

    pad = jnp.zeros((positions, EXTRA - rope), BF16)
    block = jnp.concatenate([prompt_latent[0], prompt_pos[0], pad], axis=1)
    z_block = swap(block, "zh")
    lat_part = decode_query[0, 0].reshape(steps, CTX, own_heads, lat)
    pos_part = decode_query_pos[0, 0].reshape(steps, CTX, own_heads, rope)
    queries = jnp.concatenate(
        [lat_part, pos_part, jnp.zeros((steps, CTX, own_heads, EXTRA - rope), BF16)], axis=-1
    )
    queries = queries.transpose(1, 2, 0, 3).reshape(CTX, own_heads * steps, -1)
    own = jnp.concatenate([decode_latent[0, 0], decode_pos[0, 0], pad[:steps]], axis=1)
    own = jnp.broadcast_to(own[None], (CTX, steps, own.shape[1]))
    sent = jnp.concatenate([queries, own], axis=1)
    cube = sent.reshape(2, 4, 2, *sent.shape[1:])
    near, away = [lax.dynamic_index_in_dim(cube, side, 2, False) for side in (core, 1 - core)]
    got = swap(away, "core")
    cube = jnp.where(core == 0, jnp.stack([near, got]), jnp.stack([got, near]))
    near, away = [lax.dynamic_index_in_dim(cube, side, 1, False) for side in (z_hi, 1 - z_hi)]
    cube = jnp.stack([near, swap(away, "zh")])
    pieces = [lax.dynamic_index_in_dim(cube, y ^ flip, 2, False) for flip in GRAY]
    got = jnp.stack([pieces[0], *swap_square(pieces[1:], Y_HOPS)], axis=1)
    got = got.reshape(CTX, *sent.shape[1:])
    queries = got[:, : own_heads * steps].reshape(CTX, own_heads, steps, -1)
    queries = queries.transpose(1, 0, 2, 3).reshape(own_heads * CTX * steps, -1)
    own = got[:, own_heads * steps :].reshape(CTX * steps, -1)

    hidden = decode_hidden[0, 0].astype(F32)
    named = route_ids[0, 0][:, :, None] == jnp.arange(EXTRA, dtype=jnp.int32)
    routes = jnp.sum(jnp.where(named, route_gates[0, 0].astype(F32)[:, :, None], 0.0), axis=1)
    row_core = jnp.arange(8, dtype=jnp.int32)[:, None] // steps
    injected = []
    for part in pick(core, (hidden[:, :half], hidden[:, half:])):
        rows = jnp.tile(jnp.concatenate([routes, part], axis=1), (8 // steps, 1))
        injected.append(jnp.where(row_core == core, rows, 0.0))
    inject = jnp.stack(injected)

    near_a, far_a = swap(block, "ya", "yb"), swap(z_block, "yb", "ya")
    near, far = jnp.concatenate([block, near_a]), jnp.concatenate([z_block, far_a])
    units, columns = expert_gate.shape[-1], expert_down.shape[-1]
    starts = (core * half, half - core * half)
    down = expert_down[0].T.reshape(columns, CTX, units).transpose(1, 0, 2)
    lent_in = jnp.concatenate(
        [lax.dynamic_slice_in_dim(part, starts[1], half, 0) for part in (expert_gate[0], expert_up[0])], axis=1
    )
    near, far, lent_in, down = lax.optimization_barrier((near, far, lent_in, down))
    near_b, far_b = swap(near, "yb", "ya"), swap(far, "ya", "yb")
    got_in = swap(lent_in, "core")
    near_keys = jnp.concatenate([near, near_b, far, far_b])
    tied = (near_keys, queries, own, inject)
    near_keys, queries, own, inject = lax.optimization_barrier(tied)
    keys = (near_keys, swap(near_keys, "core"))

    keep, send = decode_attention(core, queries, keys, own, inject, value_up, out_proj)

    rotary, ctx = after(send, prompt_query_pos[0], ctx)
    query_pos = rotary.reshape(positions, heads, rope)
    key_rows = (slot_blocks(z_hi, y, core)[:, None] * positions + jnp.arange(positions)[None]).reshape(-1)
    query_rows = ctx * positions + jnp.arange(positions)
    bias = jnp.where(key_rows[None, :] <= query_rows[:, None], 0.0, MASK_VALUE).astype(F32)
    state = {"next": 0, "out": None}

    def prefill_beside(start, result, count):
        count = min(count, positions // CHUNK - state["next"])
        if count == 0:
            return result
        tied, start = lax.optimization_barrier((bias, start))
        for index in range(state["next"], state["next"] + count):
            state["out"] = prefill_block(index, query, query_pos, keys, tied, state["out"])
        state["next"] += count
        result, state["out"] = lax.optimization_barrier((result, state["out"]))
        return result

    summed = keep + swap(send, "core").astype(F32)
    summed = summed.reshape(2, 4, 2 * steps, -1)
    sent = summed.astype(BF16)
    got = swap_square([sent[:, n] for n in (1, 2, 3)], Y_HOPS)
    summed = summed[:, 0] + sum(part.astype(F32) for part in got)
    sent = summed.astype(BF16)
    part = swap(sent, "zh")
    summed = summed + part[::-1].astype(F32)
    summed = summed.reshape(4 * steps, -1)
    hidden_sum = summed[:, EXTRA:]
    squares = jnp.sum(hidden_sum * hidden_sum, axis=-1, keepdims=True)
    squares = squares + swap(jnp.broadcast_to(squares, (4 * steps, EXTRA)), "core")[:, :1]
    gain, _ = pick(core, (norm_gain[:half], norm_gain[half:]))
    scale_rows = lax.rsqrt(squares / width + NORM_EPS)
    normed = hidden_sum * scale_rows * gain.astype(F32)
    tokens = jnp.concatenate([summed[:, :EXTRA], normed], axis=1).astype(BF16)

    tokens = jnp.concatenate([tokens, *swap_square([tokens] * 3, Z_HOPS)])
    tokens, query_pos, bias = lax.optimization_barrier((tokens, query_pos, bias))
    rows = tokens.shape[0]
    quarter = half // 2
    (down,) = after(tokens, down)
    down = lax.all_to_all(down, "ctx", split_axis=0, concat_axis=0, tiled=True)
    tokens = jnp.concatenate([tokens, *swap_square([tokens] * 3, SMALL_HOPS)])
    lanes = [tokens[:, : EXTRA + quarter], tokens[:, EXTRA + quarter :]]
    moved = [swap(lane, *LARGE_HOPS[0][n]) for n, lane in enumerate(lanes)]
    moved[1] = prefill_beside(lanes[1], moved[1], PREFILL_AT["gather"][0])
    lanes = [jnp.concatenate(pair) for pair in zip(lanes, moved)]
    moved = [swap(lane, *LARGE_HOPS[1][n]) for n, lane in enumerate(lanes)]
    lanes[0], down = lax.optimization_barrier((lanes[0], down))
    lent_out = lax.dynamic_slice_in_dim(down, (1 - core) * (CTX // 2), CTX // 2, 0)
    got_out = swap(lent_out, "core")
    moved[1] = prefill_beside(lanes[1], moved[1], PREFILL_AT["gather"][1])
    parts = (lanes[0], moved[0], lanes[1], moved[1])

    def turn(array, axes):
        cube = array.reshape((2, 2, 2, 2, rows, array.shape[-1]))
        return cube.transpose(axes + (4, 5)).reshape(array.shape)

    place = jnp.stack([core, expert])
    other = expert_acts(other_acts_body, (BF16,), 2 * units, (), (*parts, got_in))[0]
    other = swap(other, "core")
    weights = (expert_gate[0], expert_up[0])
    acts, shares = expert_acts(own_acts_body, (F32, F32), 2 * units, (place,), (*parts, *weights))
    acts += other.astype(F32)
    expert_hidden = (jax.nn.silu(acts[:, :units]) * acts[:, units:]).astype(BF16)
    got_hidden = swap(turn(expert_hidden, (2, 3, 0, 1)), "core")

    results = [expert_results(n, place, expert_hidden, got_hidden, down, got_out, shares) for n in range(2)]
    sends, keeps = zip(*results)
    moved = [swap(lane, *LARGE_HOPS[1][n]) for n, lane in enumerate(sends)]
    moved[1] = prefill_beside(sends[1], moved[1], PREFILL_AT["back"][0])
    lanes = [keep + part.astype(F32) for keep, part in zip(keeps, moved)]
    middle = lanes[0].shape[0] // 2
    sends = [lane[middle:].astype(BF16) for lane in lanes]
    moved = [swap(lane, *LARGE_HOPS[0][n]) for n, lane in enumerate(sends)]
    moved[1] = prefill_beside(sends[1], moved[1], PREFILL_AT["back"][1])
    routed = jnp.concatenate([lane[:middle] + part.astype(F32) for lane, part in zip(lanes, moved)], axis=1)
    for hops, count in ((SMALL_HOPS, PREFILL_AT["back"][2]), (Z_HOPS, PREFILL_AT["back"][3])):
        blocks = routed.reshape(4, -1, half)
        sent = [blocks[n].astype(BF16) for n in (1, 2, 3)]
        got = swap_square(sent, hops)
        got[2] = prefill_beside(sent[2], got[2], count)
        routed = blocks[0] + sum(part.astype(F32) for part in got)
    middle = routed.shape[0] // 2
    sent = routed[middle:].astype(BF16)
    part = prefill_beside(sent, swap(sent, "zh"), PREFILL_AT["back"][4])
    routed = routed[:middle] + part.astype(F32)
    final = (hidden_sum[: 2 * steps] + routed).astype(BF16)
    mine, other = pick(core, (final[:steps], final[steps:]))
    other = swap(other, "core")
    left, right = pick(core, (mine, other))
    decode_out = jnp.concatenate([left, right], axis=1)[None, None]
    return (state["out"][None], decode_out)


def solution(mesh):
    in_specs = (
        P("ep", "ctx", None, None),
        P("ep", "ctx", None),
        P("ep", "ctx", None),
        P("ep", "ctx", None),
        P("ep", "ctx", None, None, None),
        P("ep", "ctx", None, None),
        P("ep", "ctx", None, None),
        P("ep", "ctx", None, None),
        P("ep", "ctx", None, None),
        P(),
        P("ctx", None, None),
        P("ctx", None),
        P("ep", "ctx", None, None),
        P("ep", "ctx", None, None),
        P("ep", None, "ctx"),
        P("ep", None, "ctx"),
        P("ep", None, "ctx"),
    )
    out_specs = (P("ep", "ctx", None, None), P("ep", "ctx", None, None))
    return jax.shard_map(
        on_device, mesh=mesh, in_specs=in_specs, out_specs=out_specs, check_vma=False
    )
```

```python
import functools

import jax
import jax.numpy as jnp
from jax import lax
from jax.experimental import pallas as pl
from jax.experimental.pallas import tpu as pltpu
from jax.sharding import PartitionSpec as P

SOFTMAX_SCALE = 192.0 ** (-0.5)
MASK_VALUE = -1e30
NORM_EPS = 1e-06
ROUTE_SCALE = 2.5

CTX, EP = 16, 16
BOTH = ("ctx", "ep")
BF16, F32 = jnp.bfloat16, jnp.float32

HOPS = {
    "xa": ("x", 1),
    "xb": ("x", 3),
    "ya": ("y", 1),
    "yb": ("y", 3),
    "z1": ("z_lo", 1),
    "z2": ("z_lo", 2),
    "zh": ("z_hi", 1),
    "core": ("core", 1),
}
GRAY = (0, 1, 3, 2)
EXTRA = 128
CHUNK = 8
SMALL_HOPS = (("xa", "xb"), ("ya", "yb"))
Y_HOPS = (("ya", "ya"), ("yb", "yb"))
Z_HOPS = (("z1", "z1"), ("z2", "z2"))
LARGE_HOPS = ((("xb", "xa"), ("yb", "ya")), (("yb", "ya"), ("xb", "xa")))
PREFILL_AT = {"sum": 0, "gather": (0, 1), "back": (2, 2, 2, 1, 0)}


def place_of(device):
    ctx, ep = divmod(device, EP)
    return {"z_hi": ctx // 8, "y": ctx // 2 % 4, "core": ctx % 2, "z_lo": ep // 4, "x": ep % 4}


def device_at(place):
    ctx = (place["z_hi"] * 4 + place["y"]) * 2 + place["core"]
    return ctx * EP + place["z_lo"] * 4 + place["x"]


@functools.cache
def pairs_of(hop, other_hop):
    pairs = []
    for device in range(CTX * EP):
        place = place_of(device)
        for name in (hop if place["core"] == 0 else other_hop).split("+"):
            axis, flip = HOPS[name]
            place[axis] ^= flip
        pairs.append((device, device_at(place)))
    return tuple(pairs)


def swap(array, hop, other_hop=None):
    return lax.ppermute(array, BOTH, pairs_of(hop, other_hop or hop))


def swap_square(blocks, hops):
    both = tuple("+".join(pair) for pair in zip(*hops))
    return [swap(block, *hop) for block, hop in zip(blocks, (*hops, both))]


def dot(a, b):
    return jnp.dot(a, b, preferred_element_type=F32)


def nt_dot(a, b):
    return lax.dot_general(a, b, (((1,), (1,)), ((), ())), preferred_element_type=F32)


def prefill_body(query_ref, query_pos_ref, near_ref, far_ref, bias_ref, *rest):
    out_ref = rest[-1]
    positions, heads, lat = query_ref.shape
    rope = query_pos_ref.shape[-1]
    step = 4
    sides = (near_ref, far_ref)
    count = near_ref.shape[0]
    for start in range(0, positions, step):
        part = pl.ds(start, step)
        lat_rows = query_ref[part].reshape(step * heads, lat)
        pos_rows = query_pos_ref[part].reshape(step * heads, rope)
        scores = []
        for side, ref in enumerate(sides):
            score = nt_dot(lat_rows, ref[:, :lat]) + nt_dot(pos_rows, ref[:, lat : lat + rope])
            bias = bias_ref[part, side * count : (side + 1) * count]
            bias = jnp.broadcast_to(bias[:, None, :], (step, heads, count)).reshape(score.shape)
            scores.append(score * SOFTMAX_SCALE + bias)
        top = jnp.maximum(*[jnp.max(score, axis=-1, keepdims=True) for score in scores])
        weights = [jnp.exp(score - top) for score in scores]
        totals = sum(jnp.sum(weight, axis=-1, keepdims=True) for weight in weights)
        mix = sum(dot(weight.astype(BF16), ref[:, :lat]) for weight, ref in zip(weights, sides))
        out_ref[part] = (mix / totals).astype(BF16).reshape(step, heads, lat)


def prefill_block(index, query, query_pos, keys, bias, running):
    rows, heads, lat = query.shape
    cube = pl.BlockSpec((CHUNK, heads, lat), lambda i: (index, 0, 0))
    in_specs = [cube, pl.BlockSpec((CHUNK, heads, query_pos.shape[2]), lambda i: (index, 0, 0))]
    in_specs += [pl.BlockSpec(key.shape, lambda i: (0, 0)) for key in keys]
    in_specs.append(pl.BlockSpec((CHUNK, bias.shape[1]), lambda i: (index, 0)))
    operands = [query, query_pos, *keys, bias]
    aliases = {}
    if running is not None:
        in_specs.append(pl.BlockSpec(memory_space=pl.ANY))
        operands.append(running)
        aliases = {5: 0}
    work = CHUNK * heads * bias.shape[1]
    return pl.pallas_call(
        prefill_body,
        out_shape=jax.ShapeDtypeStruct((rows, heads, lat), BF16),
        grid=(1,),
        in_specs=in_specs,
        out_specs=cube,
        input_output_aliases=aliases,
        compiler_params=pltpu.CompilerParams(vmem_limit_bytes=32 * 2**20),
        cost_estimate=pl.CostEstimate(
            flops=2 * work * (2 * lat + query_pos.shape[2]), bytes_accessed=4 * CHUNK * heads * lat, transcendentals=work
        ),
        name="prefill_block",
    )(*operands)


def decode_body(
    core_ref, query_ref, near_ref, far_ref, own_ref, inject_ref, up_any, proj_any, keep_ref, send_ref, up_ref, proj_ref, sems
):
    up_copy = pltpu.make_async_copy(up_any, up_ref, sems.at[0])
    proj_copy = pltpu.make_async_copy(proj_any, proj_ref, sems.at[1])
    up_copy.start()
    proj_copy.start()
    heads, lat, width = up_ref.shape
    tokens = own_ref.shape[0]
    rows = heads * tokens
    query = query_ref[...]
    sides = (near_ref, far_ref)
    far = [nt_dot(query, ref[...]) * SOFTMAX_SCALE for ref in sides]
    near = nt_dot(query, own_ref[...]) * SOFTMAX_SCALE
    token = lax.broadcasted_iota(jnp.int32, (rows, tokens), 0) % tokens
    key = lax.broadcasted_iota(jnp.int32, (rows, tokens), 1)
    visible = (token // 2 == key // 2) & (key <= token)
    near = jnp.where(visible, near, MASK_VALUE)
    top = jnp.max(near, axis=-1, keepdims=True)
    for part in far:
        top = jnp.maximum(top, jnp.max(part, axis=-1, keepdims=True))
    near = jnp.where(visible, jnp.exp(near - top), 0.0)
    totals = jnp.sum(near, axis=-1, keepdims=True)
    mix = dot(near.astype(BF16), own_ref[:, :lat])
    for part, ref in zip(far, sides):
        weights = jnp.exp(part - top)
        totals += jnp.sum(weights, axis=-1, keepdims=True)
        mix += dot(weights.astype(BF16), ref[:, :lat])
    mix = (mix / totals).astype(BF16)
    up_copy.wait()
    values = [dot(mix[h * tokens : (h + 1) * tokens], up_ref[h]).astype(BF16) for h in range(heads)]
    values = jnp.concatenate(values, axis=1)
    proj_copy.wait()
    half = proj_ref.shape[1] // 2
    low, high = dot(values, proj_ref[:, :half]), dot(values, proj_ref[:, half:])
    first = core_ref[0] == 0
    mine, other = jnp.where(first, low, high), jnp.where(first, high, low)
    own_rows = inject_ref.shape[1]
    pad = jnp.zeros((tokens - own_rows, EXTRA), F32)
    for ref, values, at in ((keep_ref, mine, 0), (send_ref, other, 1)):
        add = inject_ref[at]
        ref[:, :EXTRA] = jnp.concatenate([add[:, :EXTRA], pad], axis=0).astype(ref.dtype)
        ref[:own_rows, EXTRA:] = (values[:own_rows] + add[:, EXTRA:]).astype(ref.dtype)
        ref[own_rows:, EXTRA:] = values[own_rows:].astype(ref.dtype)


def decode_attention(core, query, keys, own, inject, up, proj):
    tokens, half = own.shape[0], proj.shape[1] // 2
    vmem = pl.BlockSpec(memory_space=pltpu.VMEM)
    return pl.pallas_call(
        decode_body,
        out_shape=(
            jax.ShapeDtypeStruct((tokens, EXTRA + half), F32),
            jax.ShapeDtypeStruct((tokens, EXTRA + half), BF16),
        ),
        in_specs=[pl.BlockSpec(memory_space=pltpu.SMEM)] + [vmem] * 5 + [pl.BlockSpec(memory_space=pl.ANY)] * 2,
        out_specs=(vmem, vmem),
        scratch_shapes=[
            pltpu.VMEM(up.shape, BF16),
            pltpu.VMEM(proj.shape, BF16),
            pltpu.SemaphoreType.DMA((2,)),
        ],
        compiler_params=pltpu.CompilerParams(vmem_limit_bytes=40 * 2**20),
        cost_estimate=pl.CostEstimate(flops=10**9, bytes_accessed=6 * 10**6, transcendentals=10**5),
        name="decode_attention",
    )(core.reshape(1), query, *keys, own, inject, up, proj)


def after(value, *others):
    return lax.optimization_barrier((value, *others))[1:]


LANE_BLOCK = [b // 4 % 2 * 8 + b // 8 * 4 + b % 4 for b in range(16)]
CORE_BLOCK = [b % 4 * 4 + b // 4 for b in range(16)]


def add_lanes(lane_refs, low, high, part_ref, out_ref, blocks):
    near0, far0, near1, far1 = lane_refs
    middle = near0.shape[0]
    rows = middle // 8
    for ref, at in ((near1, 0), (far1, middle)):
        part_ref[pl.ds(at, middle)] = dot(ref[...], high)
    for ref, first in ((near0, 0), (far0, 8)):
        acts = dot(ref[:, EXTRA:], low)
        for n in range(8):
            b = first + n
            block = acts[n * rows : (n + 1) * rows] + part_ref[pl.ds(LANE_BLOCK[b] * rows, rows)]
            out_ref[pl.ds(blocks[b] * rows, rows)] = block.astype(out_ref.dtype)


def other_acts_body(*refs):
    lane_refs, (got_ref, out_ref, part_ref) = refs[:4], refs[4:]
    quarter = lane_refs[2].shape[1]
    add_lanes(lane_refs, got_ref[:quarter], got_ref[quarter:], part_ref, out_ref, CORE_BLOCK)


def own_acts_body(place_ref, *refs):
    lane_refs, (gate_ref, up_ref, out_ref, shares_ref, part_ref) = refs[:4], refs[4:]
    middle, quarter = lane_refs[2].shape
    base = pl.multiple_of(place_ref[0] * (2 * quarter), 2 * quarter)
    for ref, at in zip(lane_refs[:2], (0, middle)):
        gates = ref[:, :EXTRA].astype(F32)
        here = lax.broadcasted_iota(jnp.int32, gates.shape, 1) == place_ref[1]
        gate = jnp.sum(jnp.where(here, gates, 0.0), axis=1, keepdims=True)
        share = ROUTE_SCALE * gate / jnp.sum(gates, axis=1, keepdims=True)
        shares_ref[pl.ds(at, middle)] = jnp.broadcast_to(share, gates.shape)
    sides = []
    for start in (0, quarter):
        part = pl.ds(base + start, quarter)
        sides.append(jnp.concatenate([gate_ref[part], up_ref[part]], axis=1))
    add_lanes(lane_refs, *sides, part_ref, out_ref, range(16))


def expert_acts(body, kinds, width, scalars, arrays):
    count = 2 * arrays[0].shape[0]
    vmem, smem = (pl.BlockSpec(memory_space=space) for space in (pltpu.VMEM, pltpu.SMEM))
    return pl.pallas_call(
        body,
        out_shape=[jax.ShapeDtypeStruct((count, size), kind) for size, kind in zip((width, EXTRA), kinds)],
        in_specs=[smem] * len(scalars) + [vmem] * len(arrays),
        out_specs=[vmem] * len(kinds),
        scratch_shapes=[pltpu.VMEM((count, width), F32)],
        compiler_params=pltpu.CompilerParams(vmem_limit_bytes=24 * 2**20),
        cost_estimate=pl.CostEstimate(flops=5 * 10**8, bytes_accessed=3 * 10**6, transcendentals=0),
        name="expert_acts",
    )(*scalars, *arrays)


def results_body(lane, place_ref, hidden_ref, other_ref, down_ref, got_ref, shares_ref, send_ref, keep_ref):
    chunks, depth, units = got_ref.shape
    part = slice(lane * chunks // 2, (lane + 1) * chunks // 2)
    mine = down_ref[pl.ds(place_ref[0] * chunks + part.start, chunks // 2)].reshape(-1, units)
    theirs = got_ref[part].reshape(-1, units)
    count = hidden_ref.shape[0]
    rows, middle = count // 16, count // 2
    hidden = jnp.concatenate([hidden_ref[...], other_ref[...]], axis=1)
    result = nt_dot(hidden, jnp.concatenate([mine, theirs], axis=1))
    result = result * jnp.concatenate([shares_ref[...]] * (result.shape[1] // EXTRA), axis=1)
    for b in range(16):
        at = (LANE_BLOCK[b] if lane else b) * rows
        block = result[b * rows : (b + 1) * rows]
        if at < middle:
            keep_ref[pl.ds(at, rows)] = block
        else:
            send_ref[pl.ds(at - middle, rows)] = block.astype(BF16)


def expert_results(lane, place, hidden, other, down, got, shares):
    shape = (hidden.shape[0] // 2, got.shape[0] // 2 * got.shape[1])
    vmem = pl.BlockSpec(memory_space=pltpu.VMEM)
    return pl.pallas_call(
        functools.partial(results_body, lane),
        out_shape=(jax.ShapeDtypeStruct(shape, BF16), jax.ShapeDtypeStruct(shape, F32)),
        in_specs=[pl.BlockSpec(memory_space=pltpu.SMEM)] + [vmem] * 5,
        out_specs=(vmem, vmem),
        compiler_params=pltpu.CompilerParams(vmem_limit_bytes=24 * 2**20),
        cost_estimate=pl.CostEstimate(flops=5 * 10**8, bytes_accessed=3 * 10**6, transcendentals=0),
        name="expert_results",
    )(place, hidden, other, down, got, shares)


def pick(core, pieces):
    first = core == 0
    return jnp.where(first, pieces[0], pieces[1]), jnp.where(first, pieces[1], pieces[0])


def slot_blocks(z_hi, y, core):
    orders = jnp.array([[0, 1, 3, 2], [0, 3, 1, 2]], jnp.int32)
    blocks = []
    for flip in (0, 1):
        side = core ^ flip
        for z_flip in (0, 1):
            blocks.append(((z_hi ^ z_flip) * 4 + (y ^ orders[side ^ z_flip])) * 2 + side)
    return jnp.concatenate(blocks)


def on_device(
    prompt_query,
    prompt_query_pos,
    prompt_latent,
    prompt_pos,
    decode_query,
    decode_query_pos,
    decode_latent,
    decode_pos,
    decode_hidden,
    norm_gain,
    value_up,
    out_proj,
    route_ids,
    route_gates,
    expert_gate,
    expert_up,
    expert_down,
):
    ctx = lax.axis_index("ctx")
    z_hi, y, core = ctx // 8, ctx // 2 % 4, ctx % 2
    expert = lax.axis_index("ep")
    query = prompt_query[0]
    positions, heads, lat = query.shape
    rope = prompt_pos.shape[-1]
    width = decode_hidden.shape[-1]
    half = width // 2
    steps = decode_hidden.shape[2]
    own_heads = value_up.shape[0]

    pad = jnp.zeros((positions, EXTRA - rope), BF16)
    block = jnp.concatenate([prompt_latent[0], prompt_pos[0], pad], axis=1)
    z_block = swap(block, "zh")
    lat_part = decode_query[0, 0].reshape(steps, CTX, own_heads, lat)
    pos_part = decode_query_pos[0, 0].reshape(steps, CTX, own_heads, rope)
    queries = jnp.concatenate(
        [lat_part, pos_part, jnp.zeros((steps, CTX, own_heads, EXTRA - rope), BF16)], axis=-1
    )
    queries = queries.transpose(1, 2, 0, 3).reshape(CTX, own_heads * steps, -1)
    own = jnp.concatenate([decode_latent[0, 0], decode_pos[0, 0], pad[:steps]], axis=1)
    own = jnp.broadcast_to(own[None], (CTX, steps, own.shape[1]))
    sent = jnp.concatenate([queries, own], axis=1)
    cube = sent.reshape(2, 4, 2, *sent.shape[1:])
    near, away = [lax.dynamic_index_in_dim(cube, side, 0, False) for side in (z_hi, 1 - z_hi)]
    cube = jnp.stack([near, swap(away, "zh")])
    near, away = [lax.dynamic_index_in_dim(cube, side, 2, False) for side in (core, 1 - core)]
    got = swap(away, "core")
    cube = jnp.where(core == 0, jnp.stack([near, got], axis=1), jnp.stack([got, near], axis=1))
    pieces = [lax.dynamic_index_in_dim(cube, y ^ flip, 2, False) for flip in GRAY]
    hidden = decode_hidden[0, 0].astype(F32)
    named = route_ids[0, 0][:, :, None] == jnp.arange(EXTRA, dtype=jnp.int32)
    routes = jnp.sum(jnp.where(named, route_gates[0, 0].astype(F32)[:, :, None], 0.0), axis=1)
    row_core = jnp.arange(8, dtype=jnp.int32)[:, None] // steps
    injected = []
    for part in pick(core, (hidden[:, :half], hidden[:, half:])):
        rows = jnp.tile(jnp.concatenate([routes, part], axis=1), (8 // steps, 1))
        injected.append(jnp.where(row_core == core, rows, 0.0))
    inject = jnp.stack(injected)

    near_a, far_a = swap(block, "ya", "yb"), swap(z_block, "yb", "ya")
    near, far = jnp.concatenate([block, near_a]), jnp.concatenate([z_block, far_a])
    units, columns = expert_gate.shape[-1], expert_down.shape[-1]
    starts = (core * half, half - core * half)
    down = expert_down[0].T.reshape(columns, CTX, units).transpose(1, 0, 2)
    lent_in = jnp.concatenate(
        [lax.dynamic_slice_in_dim(part, starts[1], half, 0) for part in (expert_gate[0], expert_up[0])], axis=1
    )
    near, far, lent_in, down = lax.optimization_barrier((near, far, lent_in, down))
    near_b, far_b = swap(near, "yb", "ya"), swap(far, "ya", "yb")
    got_in = swap(lent_in, "core")
    pieces = [pieces[0], *swap_square(pieces[1:], Y_HOPS)]
    near_b, far_b, *pieces = lax.optimization_barrier((near_b, far_b, *pieces))
    near_keys = jnp.concatenate([near, near_b, far, far_b])
    keys = (near_keys, swap(near_keys, "core"))
    got = jnp.stack(pieces, axis=1)
    got = got.reshape(CTX, *sent.shape[1:])
    queries = got[:, : own_heads * steps].reshape(CTX, own_heads, steps, -1)
    queries = queries.transpose(1, 0, 2, 3).reshape(own_heads * CTX * steps, -1)
    own = got[:, own_heads * steps :].reshape(CTX * steps, -1)

    keep, send = decode_attention(core, queries, keys, own, inject, value_up, out_proj)

    rotary, ctx = after(send, prompt_query_pos[0], ctx)
    query_pos = rotary.reshape(positions, heads, rope)
    key_rows = (slot_blocks(z_hi, y, core)[:, None] * positions + jnp.arange(positions)[None]).reshape(-1)
    query_rows = ctx * positions + jnp.arange(positions)
    bias = jnp.where(key_rows[None, :] <= query_rows[:, None], 0.0, MASK_VALUE).astype(F32)
    state = {"next": 0, "out": None}

    def prefill_beside(start, result, count):
        count = min(count, positions // CHUNK - state["next"])
        if count == 0:
            return result
        tied, start = lax.optimization_barrier((bias, start))
        for index in range(state["next"], state["next"] + count):
            state["out"] = prefill_block(index, query, query_pos, keys, tied, state["out"])
        state["next"] += count
        result, state["out"] = lax.optimization_barrier((result, state["out"]))
        return result

    summed = keep + swap(send, "core").astype(F32)
    summed = summed.reshape(2, 4, 2 * steps, -1)
    sent = summed.astype(BF16)
    got = swap_square([sent[:, n] for n in (1, 2, 3)], Y_HOPS)
    summed = summed[:, 0] + sum(part.astype(F32) for part in got)
    sent = summed.astype(BF16)
    part = swap(sent, "zh")
    summed = summed + part[::-1].astype(F32)
    summed = summed.reshape(4 * steps, -1)
    hidden_sum = summed[:, EXTRA:]
    squares = jnp.sum(hidden_sum * hidden_sum, axis=-1, keepdims=True)
    squares = squares + swap(jnp.broadcast_to(squares, (4 * steps, EXTRA)), "core")[:, :1]
    gain, _ = pick(core, (norm_gain[:half], norm_gain[half:]))
    scale_rows = lax.rsqrt(squares / width + NORM_EPS)
    normed = hidden_sum * scale_rows * gain.astype(F32)
    tokens = jnp.concatenate([summed[:, :EXTRA], normed], axis=1).astype(BF16)

    tokens = jnp.concatenate([tokens, *swap_square([tokens] * 3, Z_HOPS)])
    tokens, query_pos, bias = lax.optimization_barrier((tokens, query_pos, bias))
    rows = tokens.shape[0]
    quarter = half // 2
    (down,) = after(tokens, down)
    down = lax.all_to_all(down, "ctx", split_axis=0, concat_axis=0, tiled=True)
    tokens = jnp.concatenate([tokens, *swap_square([tokens] * 3, SMALL_HOPS)])
    lanes = [tokens[:, : EXTRA + quarter], tokens[:, EXTRA + quarter :]]
    moved = [swap(lane, *LARGE_HOPS[0][n]) for n, lane in enumerate(lanes)]
    moved[1] = prefill_beside(lanes[1], moved[1], PREFILL_AT["gather"][0])
    lanes = [jnp.concatenate(pair) for pair in zip(lanes, moved)]
    moved = [swap(lane, *LARGE_HOPS[1][n]) for n, lane in enumerate(lanes)]
    lanes[0], down = lax.optimization_barrier((lanes[0], down))
    lent_out = lax.dynamic_slice_in_dim(down, (1 - core) * (CTX // 2), CTX // 2, 0)
    got_out = swap(lent_out, "core")
    moved[1] = prefill_beside(lanes[1], moved[1], PREFILL_AT["gather"][1])
    parts = (lanes[0], moved[0], lanes[1], moved[1])

    def turn(array, axes):
        cube = array.reshape((2, 2, 2, 2, rows, array.shape[-1]))
        return cube.transpose(axes + (4, 5)).reshape(array.shape)

    place = jnp.stack([core, expert])
    other = expert_acts(other_acts_body, (BF16,), 2 * units, (), (*parts, got_in))[0]
    other = swap(other, "core")
    weights = (expert_gate[0], expert_up[0])
    acts, shares = expert_acts(own_acts_body, (F32, F32), 2 * units, (place,), (*parts, *weights))
    acts += other.astype(F32)
    expert_hidden = (jax.nn.silu(acts[:, :units]) * acts[:, units:]).astype(BF16)
    got_hidden = swap(turn(expert_hidden, (2, 3, 0, 1)), "core")

    results = [expert_results(n, place, expert_hidden, got_hidden, down, got_out, shares) for n in range(2)]
    sends, keeps = zip(*results)
    moved = [swap(lane, *LARGE_HOPS[1][n]) for n, lane in enumerate(sends)]
    moved[1] = prefill_beside(sends[1], moved[1], PREFILL_AT["back"][0])
    lanes = [keep + part.astype(F32) for keep, part in zip(keeps, moved)]
    middle = lanes[0].shape[0] // 2
    sends = [lane[middle:].astype(BF16) for lane in lanes]
    moved = [swap(lane, *LARGE_HOPS[0][n]) for n, lane in enumerate(sends)]
    moved[1] = prefill_beside(sends[1], moved[1], PREFILL_AT["back"][1])
    routed = jnp.concatenate([lane[:middle] + part.astype(F32) for lane, part in zip(lanes, moved)], axis=1)
    for hops, count in ((SMALL_HOPS, PREFILL_AT["back"][2]), (Z_HOPS, PREFILL_AT["back"][3])):
        blocks = routed.reshape(4, -1, half)
        sent = [blocks[n].astype(BF16) for n in (1, 2, 3)]
        got = swap_square(sent, hops)
        got[2] = prefill_beside(sent[2], got[2], count)
        routed = blocks[0] + sum(part.astype(F32) for part in got)
    middle = routed.shape[0] // 2
    sent = routed[middle:].astype(BF16)
    part = prefill_beside(sent, swap(sent, "zh"), PREFILL_AT["back"][4])
    routed = routed[:middle] + part.astype(F32)
    final = (hidden_sum[: 2 * steps] + routed).astype(BF16)
    mine, other = pick(core, (final[:steps], final[steps:]))
    other = swap(other, "core")
    left, right = pick(core, (mine, other))
    decode_out = jnp.concatenate([left, right], axis=1)[None, None]
    return (state["out"][None], decode_out)


def solution(mesh):
    in_specs = (
        P("ep", "ctx", None, None),
        P("ep", "ctx", None),
        P("ep", "ctx", None),
        P("ep", "ctx", None),
        P("ep", "ctx", None, None, None),
        P("ep", "ctx", None, None),
        P("ep", "ctx", None, None),
        P("ep", "ctx", None, None),
        P("ep", "ctx", None, None),
        P(),
        P("ctx", None, None),
        P("ctx", None),
        P("ep", "ctx", None, None),
        P("ep", "ctx", None, None),
        P("ep", None, "ctx"),
        P("ep", None, "ctx"),
        P("ep", None, "ctx"),
    )
    out_specs = (P("ep", "ctx", None, None), P("ep", "ctx", None, None))
    return jax.shard_map(
        on_device, mesh=mesh, in_specs=in_specs, out_specs=out_specs, check_vma=False
    )
```

```python
import functools

import jax
import jax.numpy as jnp
from jax import lax
from jax.experimental import pallas as pl
from jax.experimental.pallas import tpu as pltpu
from jax.sharding import PartitionSpec as P

SOFTMAX_SCALE = 192.0 ** (-0.5)
MASK_VALUE = -1e30
NORM_EPS = 1e-06
ROUTE_SCALE = 2.5

CTX, EP = 16, 16
BOTH = ("ctx", "ep")
BF16, F32 = jnp.bfloat16, jnp.float32

HOPS = {
    "xa": ("x", 1),
    "xb": ("x", 3),
    "ya": ("y", 1),
    "yb": ("y", 3),
    "z1": ("z_lo", 1),
    "z2": ("z_lo", 2),
    "zh": ("z_hi", 1),
    "core": ("core", 1),
}
GRAY = (0, 1, 3, 2)
EXTRA = 128
CHUNK = 8
SMALL_HOPS = (("xa", "xb"), ("ya", "yb"))
Y_HOPS = (("ya", "ya"), ("yb", "yb"))
Z_HOPS = (("z1", "z1"), ("z2", "z2"))
LARGE_HOPS = ((("xb", "xa"), ("yb", "ya")), (("yb", "ya"), ("xb", "xa")))
PREFILL_AT = {"sum": 0, "gather": (0, 1), "back": (2, 2, 2, 1, 0)}


def place_of(device):
    ctx, ep = divmod(device, EP)
    return {"z_hi": ctx // 8, "y": ctx // 2 % 4, "core": ctx % 2, "z_lo": ep // 4, "x": ep % 4}


def device_at(place):
    ctx = (place["z_hi"] * 4 + place["y"]) * 2 + place["core"]
    return ctx * EP + place["z_lo"] * 4 + place["x"]


@functools.cache
def pairs_of(hop, other_hop):
    pairs = []
    for device in range(CTX * EP):
        place = place_of(device)
        for name in (hop if place["core"] == 0 else other_hop).split("+"):
            axis, flip = HOPS[name]
            place[axis] ^= flip
        pairs.append((device, device_at(place)))
    return tuple(pairs)


def swap(array, hop, other_hop=None):
    return lax.ppermute(array, BOTH, pairs_of(hop, other_hop or hop))


def swap_square(blocks, hops):
    both = tuple("+".join(pair) for pair in zip(*hops))
    return [swap(block, *hop) for block, hop in zip(blocks, (*hops, both))]


def dot(a, b):
    return jnp.dot(a, b, preferred_element_type=F32)


def nt_dot(a, b):
    return lax.dot_general(a, b, (((1,), (1,)), ((), ())), preferred_element_type=F32)


def prefill_body(query_ref, query_pos_ref, near_ref, far_ref, bias_ref, *rest):
    out_ref = rest[-1]
    positions, heads, lat = query_ref.shape
    rope = query_pos_ref.shape[-1]
    step = 4
    sides = (near_ref, far_ref)
    count = near_ref.shape[0]
    for start in range(0, positions, step):
        part = pl.ds(start, step)
        lat_rows = query_ref[part].reshape(step * heads, lat)
        pos_rows = query_pos_ref[part].reshape(step * heads, rope)
        scores = []
        for side, ref in enumerate(sides):
            score = nt_dot(lat_rows, ref[:, :lat]) + nt_dot(pos_rows, ref[:, lat : lat + rope])
            bias = bias_ref[part, side * count : (side + 1) * count]
            bias = jnp.broadcast_to(bias[:, None, :], (step, heads, count)).reshape(score.shape)
            scores.append(score * SOFTMAX_SCALE + bias)
        top = jnp.maximum(*[jnp.max(score, axis=-1, keepdims=True) for score in scores])
        weights = [jnp.exp(score - top) for score in scores]
        totals = sum(jnp.sum(weight, axis=-1, keepdims=True) for weight in weights)
        mix = sum(dot(weight.astype(BF16), ref[:, :lat]) for weight, ref in zip(weights, sides))
        out_ref[part] = (mix / totals).astype(BF16).reshape(step, heads, lat)


def prefill_block(index, query, query_pos, keys, bias, running):
    rows, heads, lat = query.shape
    cube = pl.BlockSpec((CHUNK, heads, lat), lambda i: (index, 0, 0))
    in_specs = [cube, pl.BlockSpec((CHUNK, heads, query_pos.shape[2]), lambda i: (index, 0, 0))]
    in_specs += [pl.BlockSpec(key.shape, lambda i: (0, 0)) for key in keys]
    in_specs.append(pl.BlockSpec((CHUNK, bias.shape[1]), lambda i: (index, 0)))
    operands = [query, query_pos, *keys, bias]
    aliases = {}
    if running is not None:
        in_specs.append(pl.BlockSpec(memory_space=pl.ANY))
        operands.append(running)
        aliases = {5: 0}
    work = CHUNK * heads * bias.shape[1]
    return pl.pallas_call(
        prefill_body,
        out_shape=jax.ShapeDtypeStruct((rows, heads, lat), BF16),
        grid=(1,),
        in_specs=in_specs,
        out_specs=cube,
        input_output_aliases=aliases,
        compiler_params=pltpu.CompilerParams(vmem_limit_bytes=32 * 2**20),
        cost_estimate=pl.CostEstimate(
            flops=2 * work * (2 * lat + query_pos.shape[2]), bytes_accessed=4 * CHUNK * heads * lat, transcendentals=work
        ),
        name="prefill_block",
    )(*operands)


def decode_body(
    core_ref, query_ref, near_ref, far_ref, own_ref, inject_ref, up_any, proj_any, keep_ref, send_ref, up_ref, proj_ref, sems
):
    up_copy = pltpu.make_async_copy(up_any, up_ref, sems.at[0])
    proj_copy = pltpu.make_async_copy(proj_any, proj_ref, sems.at[1])
    up_copy.start()
    proj_copy.start()
    heads, lat, width = up_ref.shape
    tokens = own_ref.shape[0]
    rows = heads * tokens
    query = query_ref[...]
    sides = (near_ref, far_ref)
    far = [nt_dot(query, ref[...]) * SOFTMAX_SCALE for ref in sides]
    near = nt_dot(query, own_ref[...]) * SOFTMAX_SCALE
    token = lax.broadcasted_iota(jnp.int32, (rows, tokens), 0) % tokens
    key = lax.broadcasted_iota(jnp.int32, (rows, tokens), 1)
    visible = (token // 2 == key // 2) & (key <= token)
    near = jnp.where(visible, near, MASK_VALUE)
    top = jnp.max(near, axis=-1, keepdims=True)
    for part in far:
        top = jnp.maximum(top, jnp.max(part, axis=-1, keepdims=True))
    near = jnp.where(visible, jnp.exp(near - top), 0.0)
    totals = jnp.sum(near, axis=-1, keepdims=True)
    mix = dot(near.astype(BF16), own_ref[:, :lat])
    for part, ref in zip(far, sides):
        weights = jnp.exp(part - top)
        totals += jnp.sum(weights, axis=-1, keepdims=True)
        mix += dot(weights.astype(BF16), ref[:, :lat])
    mix = (mix / totals).astype(BF16)
    up_copy.wait()
    values = [dot(mix[h * tokens : (h + 1) * tokens], up_ref[h]).astype(BF16) for h in range(heads)]
    values = jnp.concatenate(values, axis=1)
    proj_copy.wait()
    half = proj_ref.shape[1] // 2
    low, high = dot(values, proj_ref[:, :half]), dot(values, proj_ref[:, half:])
    first = core_ref[0] == 0
    mine, other = jnp.where(first, low, high), jnp.where(first, high, low)
    own_rows = inject_ref.shape[1]
    pad = jnp.zeros((tokens - own_rows, EXTRA), F32)
    for ref, values, at in ((keep_ref, mine, 0), (send_ref, other, 1)):
        add = inject_ref[at]
        ref[:, :EXTRA] = jnp.concatenate([add[:, :EXTRA], pad], axis=0).astype(ref.dtype)
        ref[:own_rows, EXTRA:] = (values[:own_rows] + add[:, EXTRA:]).astype(ref.dtype)
        ref[own_rows:, EXTRA:] = values[own_rows:].astype(ref.dtype)


def decode_attention(core, query, keys, own, inject, up, proj):
    tokens, half = own.shape[0], proj.shape[1] // 2
    vmem = pl.BlockSpec(memory_space=pltpu.VMEM)
    return pl.pallas_call(
        decode_body,
        out_shape=(
            jax.ShapeDtypeStruct((tokens, EXTRA + half), F32),
            jax.ShapeDtypeStruct((tokens, EXTRA + half), BF16),
        ),
        in_specs=[pl.BlockSpec(memory_space=pltpu.SMEM)] + [vmem] * 5 + [pl.BlockSpec(memory_space=pl.ANY)] * 2,
        out_specs=(vmem, vmem),
        scratch_shapes=[
            pltpu.VMEM(up.shape, BF16),
            pltpu.VMEM(proj.shape, BF16),
            pltpu.SemaphoreType.DMA((2,)),
        ],
        compiler_params=pltpu.CompilerParams(vmem_limit_bytes=40 * 2**20),
        cost_estimate=pl.CostEstimate(flops=10**9, bytes_accessed=6 * 10**6, transcendentals=10**5),
        name="decode_attention",
    )(core.reshape(1), query, *keys, own, inject, up, proj)


def after(value, *others):
    return lax.optimization_barrier((value, *others))[1:]


LANE_BLOCK = [b // 4 % 2 * 8 + b // 8 * 4 + b % 4 for b in range(16)]
CORE_BLOCK = [b % 4 * 4 + b // 4 for b in range(16)]


def add_lanes(lane_refs, low, high, part_ref, out_ref, blocks):
    near0, far0, near1, far1 = lane_refs
    middle = near0.shape[0]
    rows = middle // 8
    for ref, at in ((near1, 0), (far1, middle)):
        part_ref[pl.ds(at, middle)] = dot(ref[...], high)
    for ref, first in ((near0, 0), (far0, 8)):
        acts = dot(ref[:, EXTRA:], low)
        for n in range(8):
            b = first + n
            block = acts[n * rows : (n + 1) * rows] + part_ref[pl.ds(LANE_BLOCK[b] * rows, rows)]
            out_ref[pl.ds(blocks[b] * rows, rows)] = block.astype(out_ref.dtype)


def other_acts_body(*refs):
    lane_refs, (got_ref, out_ref, part_ref) = refs[:4], refs[4:]
    quarter = lane_refs[2].shape[1]
    add_lanes(lane_refs, got_ref[:quarter], got_ref[quarter:], part_ref, out_ref, CORE_BLOCK)


def own_acts_body(place_ref, *refs):
    lane_refs, (gate_ref, up_ref, out_ref, shares_ref, part_ref) = refs[:4], refs[4:]
    middle, quarter = lane_refs[2].shape
    base = pl.multiple_of(place_ref[0] * (2 * quarter), 2 * quarter)
    for ref, at in zip(lane_refs[:2], (0, middle)):
        gates = ref[:, :EXTRA].astype(F32)
        here = lax.broadcasted_iota(jnp.int32, gates.shape, 1) == place_ref[1]
        gate = jnp.sum(jnp.where(here, gates, 0.0), axis=1, keepdims=True)
        share = ROUTE_SCALE * gate / jnp.sum(gates, axis=1, keepdims=True)
        shares_ref[pl.ds(at, middle)] = jnp.broadcast_to(share, gates.shape)
    sides = []
    for start in (0, quarter):
        part = pl.ds(base + start, quarter)
        sides.append(jnp.concatenate([gate_ref[part], up_ref[part]], axis=1))
    add_lanes(lane_refs, *sides, part_ref, out_ref, range(16))


def expert_acts(body, kinds, width, scalars, arrays):
    count = 2 * arrays[0].shape[0]
    vmem, smem = (pl.BlockSpec(memory_space=space) for space in (pltpu.VMEM, pltpu.SMEM))
    return pl.pallas_call(
        body,
        out_shape=[jax.ShapeDtypeStruct((count, size), kind) for size, kind in zip((width, EXTRA), kinds)],
        in_specs=[smem] * len(scalars) + [vmem] * len(arrays),
        out_specs=[vmem] * len(kinds),
        scratch_shapes=[pltpu.VMEM((count, width), F32)],
        compiler_params=pltpu.CompilerParams(vmem_limit_bytes=24 * 2**20),
        cost_estimate=pl.CostEstimate(flops=5 * 10**8, bytes_accessed=3 * 10**6, transcendentals=0),
        name="expert_acts",
    )(*scalars, *arrays)


def results_body(lane, place_ref, hidden_ref, other_ref, down_ref, got_ref, shares_ref, send_ref, keep_ref):
    chunks, depth, units = got_ref.shape
    part = slice(lane * chunks // 2, (lane + 1) * chunks // 2)
    mine = down_ref[pl.ds(place_ref[0] * chunks + part.start, chunks // 2)].reshape(-1, units)
    theirs = got_ref[part].reshape(-1, units)
    count = hidden_ref.shape[0]
    rows, middle = count // 16, count // 2
    hidden = jnp.concatenate([hidden_ref[...], other_ref[...]], axis=1)
    result = nt_dot(hidden, jnp.concatenate([mine, theirs], axis=1))
    result = result * jnp.concatenate([shares_ref[...]] * (result.shape[1] // EXTRA), axis=1)
    for b in range(16):
        at = (LANE_BLOCK[b] if lane else b) * rows
        block = result[b * rows : (b + 1) * rows]
        if at < middle:
            keep_ref[pl.ds(at, rows)] = block
        else:
            send_ref[pl.ds(at - middle, rows)] = block.astype(BF16)


def expert_results(lane, place, hidden, other, down, got, shares):
    shape = (hidden.shape[0] // 2, got.shape[0] // 2 * got.shape[1])
    vmem = pl.BlockSpec(memory_space=pltpu.VMEM)
    return pl.pallas_call(
        functools.partial(results_body, lane),
        out_shape=(jax.ShapeDtypeStruct(shape, BF16), jax.ShapeDtypeStruct(shape, F32)),
        in_specs=[pl.BlockSpec(memory_space=pltpu.SMEM)] + [vmem] * 5,
        out_specs=(vmem, vmem),
        compiler_params=pltpu.CompilerParams(vmem_limit_bytes=24 * 2**20),
        cost_estimate=pl.CostEstimate(flops=5 * 10**8, bytes_accessed=3 * 10**6, transcendentals=0),
        name="expert_results",
    )(place, hidden, other, down, got, shares)


def pick(core, pieces):
    first = core == 0
    return jnp.where(first, pieces[0], pieces[1]), jnp.where(first, pieces[1], pieces[0])


def slot_blocks(z_hi, y, core):
    orders = jnp.array([[0, 1, 3, 2], [0, 3, 1, 2]], jnp.int32)
    blocks = []
    for flip in (0, 1):
        side = core ^ flip
        for z_flip in (0, 1):
            blocks.append(((z_hi ^ z_flip) * 4 + (y ^ orders[side ^ z_flip])) * 2 + side)
    return jnp.concatenate(blocks)


def on_device(
    prompt_query,
    prompt_query_pos,
    prompt_latent,
    prompt_pos,
    decode_query,
    decode_query_pos,
    decode_latent,
    decode_pos,
    decode_hidden,
    norm_gain,
    value_up,
    out_proj,
    route_ids,
    route_gates,
    expert_gate,
    expert_up,
    expert_down,
):
    ctx = lax.axis_index("ctx")
    z_hi, y, core = ctx // 8, ctx // 2 % 4, ctx % 2
    expert = lax.axis_index("ep")
    query = prompt_query[0]
    positions, heads, lat = query.shape
    rope = prompt_pos.shape[-1]
    width = decode_hidden.shape[-1]
    half = width // 2
    steps = decode_hidden.shape[2]
    own_heads = value_up.shape[0]

    pad = jnp.zeros((positions, EXTRA - rope), BF16)
    block = jnp.concatenate([prompt_latent[0], prompt_pos[0], pad], axis=1)
    z_block = swap(block, "zh")
    lat_part = decode_query[0, 0].reshape(steps, CTX, own_heads, lat)
    pos_part = decode_query_pos[0, 0].reshape(steps, CTX, own_heads, rope)
    queries = jnp.concatenate(
        [lat_part, pos_part, jnp.zeros((steps, CTX, own_heads, EXTRA - rope), BF16)], axis=-1
    )
    queries = queries.transpose(1, 2, 0, 3).reshape(CTX, own_heads * steps, -1)
    own = jnp.concatenate([decode_latent[0, 0], decode_pos[0, 0], pad[:steps]], axis=1)
    own = jnp.broadcast_to(own[None], (CTX, steps, own.shape[1]))
    sent = jnp.concatenate([queries, own], axis=1)
    cube = sent.reshape(2, 4, 2, *sent.shape[1:])
    near, away = [lax.dynamic_index_in_dim(cube, side, 0, False) for side in (z_hi, 1 - z_hi)]
    cube = jnp.stack([near, swap(away, "zh")])
    near, away = [lax.dynamic_index_in_dim(cube, side, 2, False) for side in (core, 1 - core)]
    got = swap(away, "core")
    cube = jnp.where(core == 0, jnp.stack([near, got], axis=1), jnp.stack([got, near], axis=1))
    pieces = [lax.dynamic_index_in_dim(cube, y ^ flip, 2, False) for flip in GRAY]
    hidden = decode_hidden[0, 0].astype(F32)
    named = route_ids[0, 0][:, :, None] == jnp.arange(EXTRA, dtype=jnp.int32)
    routes = jnp.sum(jnp.where(named, route_gates[0, 0].astype(F32)[:, :, None], 0.0), axis=1)
    row_core = jnp.arange(8, dtype=jnp.int32)[:, None] // steps
    injected = []
    for part in pick(core, (hidden[:, :half], hidden[:, half:])):
        rows = jnp.tile(jnp.concatenate([routes, part], axis=1), (8 // steps, 1))
        injected.append(jnp.where(row_core == core, rows, 0.0))
    inject = jnp.stack(injected)

    near_a, far_a = swap(block, "ya", "yb"), swap(z_block, "yb", "ya")
    near, far = jnp.concatenate([block, near_a]), jnp.concatenate([z_block, far_a])
    units, columns = expert_gate.shape[-1], expert_down.shape[-1]
    starts = (core * half, half - core * half)
    down = expert_down[0].T.reshape(columns, CTX, units).transpose(1, 0, 2)
    lent_in = jnp.concatenate(
        [lax.dynamic_slice_in_dim(part, starts[1], half, 0) for part in (expert_gate[0], expert_up[0])], axis=1
    )
    near, far, lent_in, down = lax.optimization_barrier((near, far, lent_in, down))
    near_b, far_b = swap(near, "yb", "ya"), swap(far, "ya", "yb")
    got_in = swap(lent_in, "core")
    pieces = [pieces[0], *swap_square(pieces[1:], Y_HOPS)]
    near_b, far_b, *pieces = lax.optimization_barrier((near_b, far_b, *pieces))
    near_keys = jnp.concatenate([near, near_b, far, far_b])
    keys = (near_keys, swap(near_keys, "core"))
    got = jnp.stack(pieces, axis=1)
    got = got.reshape(CTX, *sent.shape[1:])
    queries = got[:, : own_heads * steps].reshape(CTX, own_heads, steps, -1)
    queries = queries.transpose(1, 0, 2, 3).reshape(own_heads * CTX * steps, -1)
    own = got[:, own_heads * steps :].reshape(CTX * steps, -1)

    keep, send = decode_attention(core, queries, keys, own, inject, value_up, out_proj)

    rotary, ctx = after(send, prompt_query_pos[0], ctx)
    query_pos = rotary.reshape(positions, heads, rope)
    key_rows = (slot_blocks(z_hi, y, core)[:, None] * positions + jnp.arange(positions)[None]).reshape(-1)
    query_rows = ctx * positions + jnp.arange(positions)
    bias = jnp.where(key_rows[None, :] <= query_rows[:, None], 0.0, MASK_VALUE).astype(F32)
    state = {"next": 0, "out": None}

    def prefill_beside(start, result, count):
        count = min(count, positions // CHUNK - state["next"])
        if count == 0:
            return result
        tied, start = lax.optimization_barrier((bias, start))
        for index in range(state["next"], state["next"] + count):
            state["out"] = prefill_block(index, query, query_pos, keys, tied, state["out"])
        state["next"] += count
        result, state["out"] = lax.optimization_barrier((result, state["out"]))
        return result

    summed = keep + swap(send, "core").astype(F32)
    summed = summed.reshape(2, 4, 2 * steps, -1)
    sent = summed.astype(BF16)
    got = swap_square([sent[:, n] for n in (1, 2, 3)], Y_HOPS)
    summed = summed[:, 0] + sum(part.astype(F32) for part in got)
    sent = summed.astype(BF16)
    part = swap(sent, "zh")
    summed = summed + part[::-1].astype(F32)
    summed = summed.reshape(4 * steps, -1)
    hidden_sum = summed[:, EXTRA:]
    squares = jnp.sum(hidden_sum * hidden_sum, axis=-1, keepdims=True)
    squares = squares + swap(jnp.broadcast_to(squares, (4 * steps, EXTRA)), "core")[:, :1]
    gain, _ = pick(core, (norm_gain[:half], norm_gain[half:]))
    scale_rows = lax.rsqrt(squares / width + NORM_EPS)
    normed = hidden_sum * scale_rows * gain.astype(F32)
    tokens = jnp.concatenate([summed[:, :EXTRA], normed], axis=1).astype(BF16)

    tokens = jnp.concatenate([tokens, *swap_square([tokens] * 3, Z_HOPS)])
    tokens, query_pos, bias = lax.optimization_barrier((tokens, query_pos, bias))
    rows = tokens.shape[0]
    quarter = half // 2
    tokens = jnp.concatenate([tokens, *swap_square([tokens] * 3, SMALL_HOPS)])
    (down,) = after(tokens, down)
    down = lax.all_to_all(down, "ctx", split_axis=0, concat_axis=0, tiled=True)
    lanes = [tokens[:, : EXTRA + quarter], tokens[:, EXTRA + quarter :]]
    moved = [swap(lane, *LARGE_HOPS[0][n]) for n, lane in enumerate(lanes)]
    moved[1] = prefill_beside(lanes[1], moved[1], PREFILL_AT["gather"][0])
    lanes = [jnp.concatenate(pair) for pair in zip(lanes, moved)]
    moved = [swap(lane, *LARGE_HOPS[1][n]) for n, lane in enumerate(lanes)]
    lanes[0], down = lax.optimization_barrier((lanes[0], down))
    lent_out = lax.dynamic_slice_in_dim(down, (1 - core) * (CTX // 2), CTX // 2, 0)
    got_out = swap(lent_out, "core")
    moved[1] = prefill_beside(lanes[1], moved[1], PREFILL_AT["gather"][1])
    parts = (lanes[0], moved[0], lanes[1], moved[1])

    def turn(array, axes):
        cube = array.reshape((2, 2, 2, 2, rows, array.shape[-1]))
        return cube.transpose(axes + (4, 5)).reshape(array.shape)

    place = jnp.stack([core, expert])
    other = expert_acts(other_acts_body, (BF16,), 2 * units, (), (*parts, got_in))[0]
    other = swap(other, "core")
    weights = (expert_gate[0], expert_up[0])
    acts, shares = expert_acts(own_acts_body, (F32, F32), 2 * units, (place,), (*parts, *weights))
    acts += other.astype(F32)
    expert_hidden = (jax.nn.silu(acts[:, :units]) * acts[:, units:]).astype(BF16)
    got_hidden = swap(turn(expert_hidden, (2, 3, 0, 1)), "core")

    results = [expert_results(n, place, expert_hidden, got_hidden, down, got_out, shares) for n in range(2)]
    sends, keeps = zip(*results)
    moved = [swap(lane, *LARGE_HOPS[1][n]) for n, lane in enumerate(sends)]
    moved[1] = prefill_beside(sends[1], moved[1], PREFILL_AT["back"][0])
    lanes = [keep + part.astype(F32) for keep, part in zip(keeps, moved)]
    middle = lanes[0].shape[0] // 2
    sends = [lane[middle:].astype(BF16) for lane in lanes]
    moved = [swap(lane, *LARGE_HOPS[0][n]) for n, lane in enumerate(sends)]
    moved[1] = prefill_beside(sends[1], moved[1], PREFILL_AT["back"][1])
    routed = jnp.concatenate([lane[:middle] + part.astype(F32) for lane, part in zip(lanes, moved)], axis=1)
    for hops, count in ((SMALL_HOPS, PREFILL_AT["back"][2]), (Z_HOPS, PREFILL_AT["back"][3])):
        blocks = routed.reshape(4, -1, half)
        sent = [blocks[n].astype(BF16) for n in (1, 2, 3)]
        got = swap_square(sent, hops)
        got[2] = prefill_beside(sent[2], got[2], count)
        routed = blocks[0] + sum(part.astype(F32) for part in got)
    middle = routed.shape[0] // 2
    sent = routed[middle:].astype(BF16)
    part = prefill_beside(sent, swap(sent, "zh"), PREFILL_AT["back"][4])
    routed = routed[:middle] + part.astype(F32)
    final = (hidden_sum[: 2 * steps] + routed).astype(BF16)
    mine, other = pick(core, (final[:steps], final[steps:]))
    other = swap(other, "core")
    left, right = pick(core, (mine, other))
    decode_out = jnp.concatenate([left, right], axis=1)[None, None]
    return (state["out"][None], decode_out)


def solution(mesh):
    in_specs = (
        P("ep", "ctx", None, None),
        P("ep", "ctx", None),
        P("ep", "ctx", None),
        P("ep", "ctx", None),
        P("ep", "ctx", None, None, None),
        P("ep", "ctx", None, None),
        P("ep", "ctx", None, None),
        P("ep", "ctx", None, None),
        P("ep", "ctx", None, None),
        P(),
        P("ctx", None, None),
        P("ctx", None),
        P("ep", "ctx", None, None),
        P("ep", "ctx", None, None),
        P("ep", None, "ctx"),
        P("ep", None, "ctx"),
        P("ep", None, "ctx"),
    )
    out_specs = (P("ep", "ctx", None, None), P("ep", "ctx", None, None))
    return jax.shard_map(
        on_device, mesh=mesh, in_specs=in_specs, out_specs=out_specs, check_vma=False
    )
```
